512 devices in a mesh: dom: 128 (over z, y, core), feat: 4 (over x).
Axes of the slice: x: 4, y: 4, z: 16, core: 2. Of those that a mesh axis runs over, the one named last changes fastest.
Arguments:
- node_latent: bfloat16 [131072, 512], P(('dom', 'feat')), may hold values from -6 to 6
- edge_latent: bfloat16 [393216, 512], P(('dom', 'feat')), may hold values from -6 to 6
- weights: bfloat16 [7, 512, 512], P(None, 'feat'), may hold values from -0.1875 to 0.1875
- biases: float32 [4, 512], replicated, may hold values from -3 to 3
- gains: float32 [2, 512], replicated, may hold values from 0.1 to 1.9
- shifts: float32 [2, 512], replicated, may hold values from -3 to 3
- halo_send: int32 [128, 4, 64], P('dom'), may hold values from 0 to 1023
- halo_count: int32 [128, 4], P('dom'), may hold values from 1 to 64
- coarse_rows: int32 [128, 2], P('dom'), may hold values from 0 to 1023, as said below
- edge_send: int32 [393216], P(('dom', 'feat')), may hold values from 0 to 1535, as said below
- edge_recv: int32 [393216], P(('dom', 'feat')), may hold values from -1 to 127, as said below
- node_cot: bfloat16 [131072, 512], P(('dom', 'feat')), may hold values from -6 to 6
Outputs:
- node_out: bfloat16 [131072, 512], P(('dom', 'feat'))
- node_grad: float32 [131072, 512], P(('dom', 'feat'))
The draws below stay inside these ranges and needn't reach their ends.
Inputs may be any that keep to these rules, and one draw needn't show every extreme that they name: `halo_send`: lists to the partitions at offsets +1, -1, +2, -2 of the sender, in that order; only the first halo_count entries of a list are live. `coarse_rows`: the rows of one partition are distinct. `edge_send`: A halo row of the table is named only if its slot is live. `edge_recv`: in each aligned block of 384 slots the live slots come first.
All inputs are finite; a program needn't handle non-finite values.
Results may differ from the reference program's by a relative error of at most 0.0051.
Values may be sent and summed in bfloat16 or wider, within the bound.
A program may use at most 64 MiB of HBM per device.

```python
import jax
import jax.numpy as jnp
from jax import lax

D = 512
ROWS = 256
BLOCK = 128
EDGE_SLOTS = 384
SLOT = 64
COARSE = 2
PART_NODES = 1024
NODES = 131072
EDGES_DEV = 768
EDGES = 393216
COARSE_ALL = 256
TABLE_ROWS = 1536
N_DOM = 128
N_FEAT = 4


OFFSETS = (1, -1, 2, -2)


def shared_counts(key):
    key = jax.random.fold_in(key, 977)
    first, second, third = jax.random.split(key, 3)
    total = N_DOM * 4
    counts = jax.random.randint(first, (total,), 1, SLOT + 1)
    top_at = jax.random.randint(second, (), 0, total)
    low_at = (top_at + 1 + jax.random.randint(third, (), 0, total - 1)) % total
    counts = counts.at[top_at].set(SLOT).at[low_at].set(1)
    return counts.reshape(N_DOM, 4).astype(jnp.int32)


def draw_halo_count(key, part):
    return shared_counts(key)


def draw_edge_send(key, part):
    counts = shared_counts(key)
    key = jax.random.fold_in(key, 23)
    keys = jax.random.split(key, 5)
    partition = jnp.arange(EDGES, dtype=jnp.int32) // (EDGES_DEV * N_FEAT)
    kinds = jax.random.randint(keys[0], (EDGES,), 0, 10)
    own_rows = jax.random.randint(keys[1], (EDGES,), 0, PART_NODES)
    order = jax.random.randint(keys[2], (EDGES,), 0, 4)
    offset_table = jnp.array(OFFSETS, dtype=jnp.int32)
    source = (partition - offset_table[order]) % N_DOM
    live_count = counts[source, order]
    slot_pick = jax.random.randint(keys[3], (EDGES,), 0, live_count)
    halo_rows = PART_NODES + order * SLOT + slot_pick
    coarse_pick = PART_NODES + 4 * SLOT + jax.random.randint(keys[4], (EDGES,), 0, COARSE * N_DOM)
    chosen = jnp.where(kinds < 5, own_rows, jnp.where(kinds < 8, halo_rows, coarse_pick))
    chosen = chosen.at[0].set(PART_NODES + 4 * SLOT + COARSE * N_DOM - 1).at[1].set(0)
    return chosen.astype(jnp.int32)


def draw_edge_recv(key, part):
    key = jax.random.fold_in(key, 37)
    first, second = jax.random.split(key)
    blocks = EDGES // EDGE_SLOTS
    live = jax.random.randint(first, (blocks, 1), EDGE_SLOTS // 2, EDGE_SLOTS + 1)
    target = jax.random.randint(second, (blocks, EDGE_SLOTS), 0, BLOCK)
    slot_iota = jnp.arange(EDGE_SLOTS, dtype=jnp.int32)[None, :]
    result = jnp.where(slot_iota < live, target, -1)
    result = result.at[0, 0].set(BLOCK - 1).at[0, EDGE_SLOTS - 1].set(-1)
    return result.reshape(EDGES).astype(jnp.int32)


def draw_coarse_rows(key, part):
    key = jax.random.fold_in(key, 51)
    first, second, third = jax.random.split(key, 3)
    scores = jax.random.randint(first, (N_DOM, PART_NODES), 0, 2 ** 14) * PART_NODES
    scores = scores + jnp.arange(PART_NODES, dtype=jnp.int32)[None, :]
    far_part = jax.random.randint(second, (), 0, N_DOM)
    near_part = jax.random.randint(third, (), 0, N_DOM)
    scores = scores.at[far_part, PART_NODES - 1].set(-1).at[near_part, 0].set(-1)
    picked = jnp.argsort(scores, axis=1, stable=True)[:, :COARSE]
    return picked.astype(jnp.int32)


def plant(values, own_key, smallest, largest):
    place = [jax.random.randint(jax.random.fold_in(own_key, axis), (), 0, length) for axis, length in enumerate(values.shape)]
    longest = values.shape.index(max(values.shape))
    neighbour = place[:longest] + [(place[longest] + 1) % values.shape[longest]] + place[longest + 1:]
    return values.at[tuple(place)].set(smallest).at[tuple(neighbour)].set(largest)


def block_levels(own_key, extent, shards, low, largest):
    gain = 1.0
    for axis_at, blocks in shards:
        steps = jax.random.uniform(jax.random.fold_in(jax.random.fold_in(own_key, 6), axis_at), (blocks,), jnp.float32, low / len(shards), largest / len(shards))
        gain = gain * jnp.repeat(jnp.exp(steps), extent[axis_at] // blocks).reshape((-1,) + (1,) * (len(extent) - 1 - axis_at))
    return gain


def noise(own_key, extent, deviation, most, pieces=(), held_as=jnp.bfloat16):
    values = deviation * jax.random.normal(own_key, extent, jnp.float32)
    if pieces:
        values = values * block_levels(own_key, extent, pieces, -0.22, 0.18)
    return jnp.clip(values, -most, most).astype(held_as)


def setup_inputs(seed: int = 0) -> dict:
    seeds = jax.random.split(jax.random.key(seed), 13)
    node_latent = noise(seeds[0], (NODES, D), 1.0, 6.0, ((0, 512),))
    edge_latent = noise(seeds[1], (EDGES, D), 1.0, 6.0, ((0, 512),))
    weights = noise(seeds[2], (7, D, D), (2 * D) ** -0.5, 0.1875, ((1, 4),))
    biases = noise(seeds[3], (4, D), 0.5, 3.0, (), jnp.float32)
    gains = jnp.clip(1.0 + 0.18 * jax.random.normal(seeds[4], (2, D), jnp.float32), 0.1, 1.9)
    shifts = noise(seeds[5], (2, D), 0.5, 3.0, (), jnp.float32)
    halo_send = plant(jax.random.randint(seeds[6], (N_DOM, 4, SLOT), 0, PART_NODES), jax.random.fold_in(seeds[6], 1), 0, PART_NODES - 1).astype(jnp.int32)
    halo_count = draw_halo_count(jax.random.fold_in(seeds[12], 71), 0)
    coarse_rows = draw_coarse_rows(jax.random.fold_in(seeds[12], 71), 0)
    edge_send = draw_edge_send(jax.random.fold_in(seeds[12], 71), 0)
    edge_recv = draw_edge_recv(jax.random.fold_in(seeds[12], 71), 0)
    node_cot = noise(seeds[11], (NODES, D), 1.0, 6.0, ((0, 512),))
    return {"node_latent": node_latent, "edge_latent": edge_latent, "weights": weights, "biases": biases, "gains": gains, "shifts": shifts, "halo_send": halo_send, "halo_count": halo_count, "coarse_rows": coarse_rows, "edge_send": edge_send, "edge_recv": edge_recv, "node_cot": node_cot}


OFFSETS = (1, -1, 2, -2)
epsilon = 1e-05

def product(left, right):
    return jnp.dot(left, right, preferred_element_type=jnp.float32)

def silu_slope(values):
    sigmoid = jax.nn.sigmoid(values)
    return sigmoid * (1.0 + values * (1.0 - sigmoid))

def norm_forward(values, gain_row, shift_row):
    centre = lax.optimization_barrier(jnp.mean(values, axis=-1, keepdims=True))
    centred = values - centre
    inv_std = lax.rsqrt(lax.optimization_barrier(jnp.mean(centred * centred, axis=-1, keepdims=True)) + epsilon)
    normed = centred * inv_std
    return (normed * gain_row + shift_row, normed, inv_std)

def norm_backward(upstream, normed, inv_std, gain_row):
    scaled = upstream * gain_row
    return inv_std * (scaled - lax.optimization_barrier(jnp.mean(scaled, axis=-1, keepdims=True)) - normed * lax.optimization_barrier(jnp.mean(scaled * normed, axis=-1, keepdims=True)))

def reference(node_latent, edge_latent, weights, biases, gains, shifts, halo_send, halo_count, coarse_rows, edge_send, edge_recv, node_cot):
    w_edge = weights[0]
    w_send = weights[1]
    w_recv = weights[2]
    w_second = weights[3]
    w_node = weights[4]
    w_agg = weights[5]
    w_last = weights[6]
    send_proj = product(node_latent, w_send).astype(jnp.bfloat16)
    recv_proj = product(node_latent, w_recv).astype(jnp.bfloat16)
    dom_iota = jnp.arange(N_DOM, dtype=jnp.int32)
    slot_iota = jnp.arange(SLOT, dtype=jnp.int32)
    id_parts = [dom_iota[:, None] * PART_NODES + jnp.arange(PART_NODES, dtype=jnp.int32)[None, :]]
    live_parts = [jnp.ones((N_DOM, PART_NODES), jnp.bool_)]
    for order in range(4):
        source = (dom_iota - OFFSETS[order]) % N_DOM
        id_parts.append(source[:, None] * PART_NODES + halo_send[source, order])
        live_parts.append(slot_iota[None, :] < halo_count[source, order][:, None])
    coarse_ids = (dom_iota[:, None] * PART_NODES + coarse_rows).reshape(1, COARSE_ALL)
    id_parts.append(jnp.broadcast_to(coarse_ids, (N_DOM, COARSE_ALL)).astype(jnp.int32))
    live_parts.append(jnp.ones((N_DOM, COARSE_ALL), jnp.bool_))
    table_ids = jnp.concatenate(id_parts, axis=1).astype(jnp.int32)
    table_live = jnp.concatenate(live_parts, axis=1)
    edge_iota = jnp.arange(N_FEAT * EDGES_DEV, dtype=jnp.int32)
    member = edge_iota // EDGES_DEV
    block_base = member * ROWS + edge_iota % EDGES_DEV // EDGE_SLOTS * BLOCK

    def partition(inputs):
        ids, live, nodes, edges, senders, receivers, cotangent, recv_rows = inputs
        table = jnp.where(live[:, None], send_proj[ids], jnp.zeros((), jnp.bfloat16))
        edge_live = receivers >= 0
        target = (block_base + jnp.maximum(receivers, 0)).astype(jnp.int32)
        recv_term = jnp.where(edge_live[:, None], recv_rows[target], jnp.zeros((), jnp.bfloat16)).astype(jnp.float32)
        hidden_in = product(edges, w_edge) + table[senders].astype(jnp.float32) + recv_term + biases[0]
        edge_act = jax.nn.silu(hidden_in).astype(jnp.bfloat16)
        edge_pre = product(edge_act, w_second) + biases[1]
        message_full, edge_normed, edge_inv = norm_forward(edge_pre, gains[0], shifts[0])
        message = message_full.astype(jnp.bfloat16)
        aggregate = jax.ops.segment_sum(jnp.where(edge_live[:, None], message.astype(jnp.float32), 0.0), target, num_segments=PART_NODES).astype(jnp.bfloat16)
        node_in = product(nodes, w_node) + product(aggregate, w_agg) + biases[2]
        node_act = jax.nn.silu(node_in).astype(jnp.bfloat16)
        node_pre = product(node_act, w_last) + biases[3]
        update, node_normed, node_inv = norm_forward(node_pre, gains[1], shifts[1])
        node_out = (nodes.astype(jnp.float32) + update).astype(jnp.bfloat16)
        cot_float = cotangent.astype(jnp.float32)
        node_back = norm_backward(cot_float, node_normed, node_inv, gains[1]).astype(jnp.bfloat16)
        node_in_grad = (product(node_back, w_last.T) * silu_slope(node_in)).astype(jnp.bfloat16)
        agg_grad = product(node_in_grad, w_agg.T).astype(jnp.bfloat16)
        message_grad = jnp.where(edge_live[:, None], agg_grad[target], jnp.zeros((), jnp.bfloat16)).astype(jnp.float32)
        edge_back = norm_backward(message_grad, edge_normed, edge_inv, gains[0]).astype(jnp.bfloat16)
        hidden_grad = (product(edge_back, w_second.T) * silu_slope(hidden_in)).astype(jnp.bfloat16)
        hidden_float = hidden_grad.astype(jnp.float32)
        table_grad = jax.ops.segment_sum(hidden_float, senders, num_segments=TABLE_ROWS)
        recv_grad = jax.ops.segment_sum(jnp.where(edge_live[:, None], hidden_float, 0.0), target, num_segments=PART_NODES).astype(jnp.bfloat16)
        base_grad = cot_float + product(node_in_grad, w_node.T)
        return (node_out, base_grad, product(recv_grad, w_recv.T), table_grad)
    node_out, base_grad, recv_part, table_grad = lax.map(partition, (table_ids, table_live, node_latent.reshape(N_DOM, PART_NODES, D), edge_latent.reshape(N_DOM, N_FEAT * EDGES_DEV, D), edge_send.reshape(N_DOM, N_FEAT * EDGES_DEV), edge_recv.reshape(N_DOM, N_FEAT * EDGES_DEV), node_cot.reshape(N_DOM, PART_NODES, D), recv_proj.reshape(N_DOM, PART_NODES, D)))
    send_grad = jax.ops.segment_sum(jnp.where(table_live.reshape(-1)[:, None], table_grad.reshape(-1, D), 0.0), table_ids.reshape(-1), num_segments=NODES).astype(jnp.bfloat16)
    node_grad = base_grad.reshape(NODES, D) + product(send_grad, w_send.T) + recv_part.reshape(NODES, D)
    return (node_out.reshape(NODES, D), node_grad)
```

```python
import jax
import jax.numpy as jnp
from jax import lax
from jax.experimental import pallas as pl
from jax.experimental.pallas import tpu as pltpu
from jax.sharding import PartitionSpec as P

MESH = pl.DeviceIdType.MESH
F32, BF16 = jnp.float32, jnp.bfloat16
D = 512
ROWS = 256
EDGES = 768
BLOCK = 128
SLOTS = 384
PART = 1024
HALO = 256
COARSE = 256
TABLE = PART + HALO + COARSE
OFFSETS = (1, -1, 2, -2)
NZ, NY, NX = 16, 4, 4
GROUPS = ((0, 3), (3, 4))
EPS = 1e-05

COUNTS = dict(c1=3, w1=12, lat=3, c2=15, w2=12, halo=4, w3=4, c3=7, hb=4, rs=3, rc1=7, rc2=15, rc3=3)
BASE = {}
_total = 0
for _name, _n in COUNTS.items():
    BASE[_name] = _total
    _total += _n
N_SEM = _total


def dot(a, b):
    return jnp.dot(a, b, preferred_element_type=F32)


def dot_t(a, b):
    return lax.dot_general(a, b, (((1,), (1,)), ((), ())), preferred_element_type=F32)


def sigmoid(v):
    return 1.0 / (1.0 + jnp.exp(-v))


def onehot(mask):
    return jnp.where(mask, 1.0, 0.0).astype(BF16)


def iota(shape, dim):
    return lax.broadcasted_iota(jnp.int32, shape, dim)


def columns(row):
    wide = jnp.broadcast_to(row.astype(F32), (128, row.shape[1]))
    return wide.T.astype(jnp.int32)


def norm(values):
    centred = values - jnp.mean(values, axis=-1, keepdims=True)
    inv = lax.rsqrt(jnp.mean(centred * centred, axis=-1, keepdims=True) + EPS)
    return centred * inv, inv


def norm_back(scaled, normed, inv):
    return inv * (
        scaled
        - jnp.mean(scaled, axis=-1, keepdims=True)
        - normed * jnp.mean(scaled * normed, axis=-1, keepdims=True)
    )


def kernel(
    coarse_ref, count_ref, node_ref, edge_ref, wsh_ref, bias_ref, gain_ref, shift_ref,
    halo_ref, esend_ref, erecv_ref, cot_ref,
    out_ref, grad_ref,
    lat, tab, w, sel, sel_t, rsel, rsel_t, hid, normed_e, inv_e, msg, hg,
    c1_src, c1_buf, c2_src, c2_buf, c3_src, halo_src, hb_src, hb_buf, part_src, rs_buf,
    rc1_src, rc1_buf, rc2_src, rc2_buf, rc3_src, rc3_buf,
    send_sem, recv_sem, local_sem,
):
    dom, x = lax.axis_index("dom"), lax.axis_index("feat")
    z, y, c = dom // 8, (dom // 2) % 4, dom % 2
    yc = dom % 8
    zm = z % 4

    def at_x(d):
        return (dom, (x + d) % NX)

    def at_z(d):
        return (((z + d + NZ) % NZ) * 8 + yc, x)

    def at_y(d):
        return (z * 8 + ((y + d) % NY) * 2 + c, x)

    def at_yc(e):
        return (z * 8 + (yc + e) % 8, x)

    def at_dom(o):
        return ((dom + o + 128) % 128, x)

    other_core = (z * 8 + y * 2 + (1 - c), x)

    def copy(name, number, src, dst, device):
        at = BASE[name] + number
        return pltpu.make_async_remote_copy(
            src_ref=src, dst_ref=dst, send_sem=send_sem.at[at], recv_sem=recv_sem.at[at],
            device_id=device, device_id_type=MESH,
        )

    barrier = pltpu.get_barrier_semaphore()
    for d in (1, 2, 3):
        pl.semaphore_signal(barrier, inc=1, device_id=at_x(d), device_id_type=MESH)
    for e in range(1, 8):
        pl.semaphore_signal(barrier, inc=1, device_id=at_yc(e), device_id_type=MESH)
    for o in OFFSETS:
        pl.semaphore_signal(barrier, inc=1, device_id=at_dom(o), device_id_type=MESH)

    def greet(d, carry):
        pl.semaphore_signal(barrier, inc=1, device_id=at_z(d), device_id_type=MESH)
        return carry

    lax.fori_loop(1, NZ, greet, 0)

    row8 = iota((8, ROWS), 0)
    wanted = jnp.where(row8 % 2 == 0, coarse_ref[0, 0], coarse_ref[0, 1]) - x * ROWS
    picked = dot(onehot(wanted == iota((8, ROWS), 1)), node_ref[...])
    quarter = iota((8, 128), 0) // 2
    tile = jnp.zeros((8, 128), F32)
    for j in range(4):
        tile = jnp.where(quarter == j, picked[:, 128 * j : 128 * j + 128], tile)
    c1_src[...] = tile

    own_rows = pl.ds(pl.multiple_of(x * ROWS, ROWS), ROWS)
    lat[own_rows, :] = node_ref[...]
    pl.semaphore_wait(barrier, 3 + 7 + 4 + 15)

    c1 = [copy("c1", d - 1, c1_src, c1_buf.at[d - 1], at_x(d)) for d in (1, 2, 3)]
    for one in c1:
        one.start()
    pieces = ((y, 0), (zm, 1))
    w1 = {}
    for g, (first, count) in enumerate(GROUPS):
        mats = pl.ds(first, count)
        for t, (j, _) in enumerate(pieces):
            cols = pl.ds(256 * t, 256)
            for d in (2, 1, 3):
                w1[g, t, d] = copy(
                    "w1", (g * 2 + t) * 3 + d - 1,
                    wsh_ref.at[mats, j, c, :, cols], w.at[mats, x, j, c, :, cols], at_x(d),
                )
                w1[g, t, d].start()
    lat_copies = [copy("lat", d - 1, node_ref, lat.at[own_rows, :], at_x(d)) for d in (2, 1, 3)]
    for one in lat_copies:
        one.start()
    for t, (j, _) in enumerate(pieces):
        cols = pl.ds(256 * t, 256)
        own = pltpu.make_async_copy(
            wsh_ref.at[:, j, c, :, cols], w.at[:, x, j, c, :, cols], local_sem.at[t]
        )
        own.start()
        own.wait()

    halo_row = halo_ref[...]
    lane = iota((1, HALO), 1)
    live = count_ref[0, 0]
    for k in (1, 2, 3):
        live = jnp.where(lane // 64 == k, count_ref[0, k], live)
    halo_row = jnp.where(lane % 64 < live, halo_row, -1)
    halo_col = columns(halo_row)

    for one in c1:
        one.wait_recv()
    total = c1_src[...] + c1_buf[0] + c1_buf[1] + c1_buf[2]
    c2_src[...] = total
    c2_buf[z] = total

    def c2(d):
        at = BASE["c2"] + d - 1
        return pltpu.make_async_remote_copy(
            src_ref=c2_src, dst_ref=c2_buf.at[z],
            send_sem=send_sem.at[at], recv_sem=recv_sem.at[at],
            device_id=at_z(d), device_id_type=MESH,
        )

    order = [8]
    for i in range(1, 8):
        order += [8 - i, 8 + i]
    for d in order:
        c2(d).start()

    index = esend_ref[...]
    m = index - (PART + HALO)
    index = jnp.where(
        m >= 0, PART + HALO + ((m >> 1) & 7) * 32 + (m >> 4) * 2 + (m & 1), index
    )

    def w2_start(g):
        first, count = GROUPS[g]
        mats = pl.ds(first, count)
        started = []
        for t, (j, _) in enumerate(pieces):
            cols = pl.ds(256 * t, 256)
            for d in (1, 2, 3):
                w1[g, t, d].wait_recv()
            for d in (2, 1, 3):
                step = d if d < 3 else -1
                target = at_y(d) if t == 0 else at_z(step)
                part = w.at[mats, :, j, c, :, cols]
                one = copy("w2", (g * 2 + t) * 3 + d - 1, part, part, target)
                one.start()
                started.append(one)
        return started

    def w3_start(g, arrived):
        first, count = GROUPS[g]
        mats = pl.ds(first, count)
        started = []
        for t in range(2):
            for one in arrived[3 * t : 3 * t + 3]:
                one.wait_recv()
            part = w.at[mats, :, :, c, :, pl.ds(256 * t, 256)]
            one = copy("w3", g * 2 + t, part, part, other_core)
            one.start()
            started.append(one)
        return started

    w2a = w2_start(0)
    index_col = columns(index)
    for j in range(TABLE // 128):
        sel[:, 128 * j : 128 * j + 128] = onehot(index_col == iota((EDGES, 128), 1) + 128 * j)
    w2b = w2_start(1)
    recv_row = erecv_ref[...]
    recv_col = columns(recv_row)
    rsel[...] = onehot(recv_col == iota((EDGES, 128), 1))
    for b in range(2):
        rsel_t[b] = onehot(
            iota((BLOCK, SLOTS), 0) == recv_row[:, SLOTS * b : SLOTS * b + SLOTS]
        )

    w3a = w3_start(0, w2a)
    for one in lat_copies:
        one.wait_recv()
    chosen = jnp.zeros((HALO, D), F32)
    for j in range(2):
        pick = jnp.concatenate(
            [onehot(halo_col == iota((HALO, 128), 1) + 128 * (4 * j + i)) for i in range(4)], axis=1
        )
        chosen += dot(pick, lat[512 * j : 512 * j + 512, :])
    halo_src[...] = chosen.astype(BF16)
    halo_copies = []
    for k in range(4):
        one = copy(
            "halo", k, halo_src.at[pl.ds(64 * k, 64)], lat.at[pl.ds(PART + 64 * k, 64)], at_dom(OFFSETS[k])
        )
        one.start()
        halo_copies.append(one)

    for d in order:
        c2(d).wait_recv()
    flat = c2_buf[...].reshape(NZ * 8, 128).astype(BF16)
    parts = []
    for j in range(4):
        row = iota((32, 128), 0)
        parts.append(dot(onehot((row // 2) * 8 + 2 * j + row % 2 == iota((32, 128), 1)), flat))
    own_coarse = jnp.concatenate(parts, axis=1).astype(BF16)
    c3_src[...] = own_coarse
    coarse_rows = pl.ds(pl.multiple_of(PART + HALO + yc * 32, 32), 32)
    lat[coarse_rows, :] = own_coarse
    c3 = [copy("c3", e - 1, c3_src, lat.at[coarse_rows, :], at_yc(e)) for e in range(1, 8)]
    for one in c3:
        one.start()
    w3b = w3_start(1, w2b)

    def weight(i):
        return w[i].reshape(D, D)

    for one in w3a:
        one.wait_recv()
    w_e, w_s, w_r = weight(0), weight(1), weight(2)
    recv_proj = dot(node_ref[...], w_r).astype(BF16)
    for j in range(4):
        rows = slice(256 * j, 256 * j + 256)
        tab[rows, :] = dot(lat[rows, :], w_s).astype(BF16)
    for b in range(2):
        rows = slice(SLOTS * b, SLOTS * b + SLOTS)
        hid[rows, :] = (
            dot(edge_ref[rows, :], w_e)
            + dot(rsel[rows, :], recv_proj[BLOCK * b : BLOCK * b + BLOCK])
            + dot(sel[rows, :PART], tab[:PART, :])
            + bias_ref[0:1, :]
        )
    for j in range(TABLE // 128):
        sel_t[128 * j : 128 * j + 128, :] = onehot(iota((128, EDGES), 0) + 128 * j == index)
    for one in halo_copies:
        one.wait_recv()
    rows = slice(PART, PART + HALO)
    tab[rows, :] = dot(lat[rows, :], w_s).astype(BF16)
    for one in c3:
        one.wait_recv()
    rows = slice(PART + HALO, TABLE)
    tab[rows, :] = dot(lat[rows, :], w_s).astype(BF16)

    for one in w3b:
        one.wait_recv()
    aggregate = []
    for b in range(2):
        rows = slice(SLOTS * b, SLOTS * b + SLOTS)
        h = hid[rows, :] + dot(sel[rows, PART:], tab[PART:, :])
        hid[rows, :] = h
        act = (h * sigmoid(h)).astype(BF16)
        normed, inv = norm(dot(act, weight(3)) + bias_ref[1:2, :])
        normed_e[rows, :] = normed
        inv_e[rows, :] = inv
        msg[rows, :] = (normed * gain_ref[0:1, :] + shift_ref[0:1, :]).astype(BF16)
        aggregate.append(dot(rsel_t[b], msg[rows, :]).astype(BF16))
    aggregate = jnp.concatenate(aggregate, axis=0)
    node = node_ref[...]
    node_in = dot(node, weight(4)) + dot(aggregate, weight(5)) + bias_ref[2:3, :]
    s = sigmoid(node_in)
    slope = s * (1.0 + node_in * (1.0 - s))
    normed, inv = norm(dot((node_in * s).astype(BF16), weight(6)) + bias_ref[3:4, :])
    out_ref[...] = (
        node.astype(F32) + (normed * gain_ref[1:2, :] + shift_ref[1:2, :])
    ).astype(BF16)
    cot = cot_ref[...].astype(F32)
    node_back = norm_back(cot * gain_ref[1:2, :], normed, inv).astype(BF16)
    node_in_grad = (dot_t(node_back, weight(6)) * slope).astype(BF16)
    agg_grad = dot_t(node_in_grad, weight(5)).astype(BF16)
    for b in range(2):
        rows = slice(SLOTS * b, SLOTS * b + SLOTS)
        back = dot(rsel[rows, :], agg_grad[BLOCK * b : BLOCK * b + BLOCK])
        edge_back = norm_back(back * gain_ref[0:1, :], normed_e[rows, :], inv_e[rows, :]).astype(BF16)
        h = hid[rows, :]
        s = sigmoid(h)
        hg[rows, :] = (dot_t(edge_back, weight(3)) * (s * (1.0 + h * (1.0 - s)))).astype(BF16)

    rc1_src[...] = dot(sel_t[PART + HALO :, :], hg[...]).astype(BF16)
    rc1 = [
        copy(
            "rc1", e - 1,
            rc1_src.at[pl.ds(pl.multiple_of((yc + e) % 8 * 32, 32), 32)], rc1_buf.at[e - 1], at_yc(e),
        )
        for e in range(1, 8)
    ]
    for one in rc1:
        one.start()
    hb_src[...] = dot(sel_t[PART : PART + HALO, :], hg[...]).astype(BF16)
    hb = []
    for k in range(4):
        part = pl.ds(64 * k, 64)
        hb.append(copy("hb", k, hb_src.at[part], hb_buf.at[part], at_dom(-OFFSETS[k])))
        hb[-1].start()

    recv_grad = [
        dot(rsel_t[b], hg[SLOTS * b : SLOTS * b + SLOTS, :]).astype(BF16) for b in range(2)
    ]
    grad_ref[...] = (
        cot_ref[...].astype(F32)
        + dot_t(node_in_grad, weight(4))
        + dot_t(jnp.concatenate(recv_grad, axis=0), weight(2))
    )

    for one in rc1:
        one.wait_recv()
    gathered = rc1_src[pl.ds(pl.multiple_of(yc * 32, 32), 32), :].astype(F32)
    for e in range(7):
        gathered += rc1_buf[e].astype(F32)
    gathered = gathered.astype(BF16)
    spread = jnp.zeros((NZ * 8, 128), F32)
    for j in range(4):
        row, col = iota((NZ * 8, 32), 0), iota((NZ * 8, 32), 1)
        place = (row // 8 == col // 2) & (row % 8 == 2 * j + col % 2)
        spread += dot(onehot(place), gathered[:, 128 * j : 128 * j + 128])
    rc2_src[...] = spread.reshape(NZ, 8, 128)
    rc2_buf[z] = rc2_src[z]

    def rc2(d):
        at = BASE["rc2"] + d - 1
        return pltpu.make_async_remote_copy(
            src_ref=rc2_src.at[(z + d) % NZ], dst_ref=rc2_buf.at[z],
            send_sem=send_sem.at[at], recv_sem=recv_sem.at[at],
            device_id=at_z(d), device_id_type=MESH,
        )

    for d in order:
        rc2(d).start()

    for one in hb:
        one.wait_recv()
    rs = []
    for d in (2, 1, 3, 0):
        start_row = pl.multiple_of(((x + d) % NX) * ROWS, ROWS)
        chunk = pl.ds(start_row, ROWS)
        place = onehot(iota((ROWS, HALO), 0) + start_row == halo_row)
        value = dot(sel_t[chunk, :], hg[...]) + dot(place, hb_buf[...])
        if d:
            part_src[d - 1] = value.astype(BF16)
            rs.append(copy("rs", d - 1, part_src.at[d - 1], rs_buf.at[d - 1], at_x(d)))
            rs[-1].start()
        else:
            hid[:ROWS, :] = value

    for d in order:
        rc2(d).wait_recv()
    tile = jnp.sum(rc2_buf[...], axis=0)
    rc3_src[...] = tile
    rc3 = [copy("rc3", d - 1, rc3_src, rc3_buf.at[d - 1], at_x(d)) for d in (1, 2, 3)]
    for one in rc3:
        one.start()
    for one in rc3:
        one.wait_recv()
    tile = rc3_src[...] + rc3_buf[0] + rc3_buf[1] + rc3_buf[2]
    for one in rs:
        one.wait_recv()
    value = hid[:ROWS, :]
    for d in range(3):
        value += rs_buf[d].astype(F32)
    for i in range(2):
        line = jnp.concatenate([tile[2 * j + i : 2 * j + i + 1, :] for j in range(4)], axis=1)
        here = iota((ROWS, D), 0) + x * ROWS == coarse_ref[0, i]
        value += jnp.where(here, line, 0.0)
    grad_ref[...] += dot_t(value.astype(BF16), weight(1))

    for one in c1 + list(w1.values()) + lat_copies + w2a + w2b + w3a + w3b:
        one.wait_send()
    for one in halo_copies + c3 + rc1 + hb + rs + rc3:
        one.wait_send()
    for d in order:
        c2(d).wait_send()
        rc2(d).wait_send()


def body(node, edge, weights, biases, gains, shifts, halo_send, halo_count, coarse, esend, erecv, cot):
    vmem = pl.BlockSpec(memory_space=pltpu.VMEM)
    smem = pl.BlockSpec(memory_space=pltpu.SMEM)
    return pl.pallas_call(
        kernel,
        name="layer",
        out_shape=(
            jax.ShapeDtypeStruct((ROWS, D), BF16),
            jax.ShapeDtypeStruct((ROWS, D), F32),
        ),
        in_specs=[smem, smem] + [vmem] * 10,
        out_specs=(vmem, vmem),
        scratch_shapes=[
            pltpu.VMEM((TABLE, D), BF16),
            pltpu.VMEM((TABLE, D), BF16),
            pltpu.VMEM((7, NX, 4, 2, 16, D), BF16),
            pltpu.VMEM((EDGES, TABLE), BF16),
            pltpu.VMEM((TABLE, EDGES), BF16),
            pltpu.VMEM((EDGES, BLOCK), BF16),
            pltpu.VMEM((2, BLOCK, SLOTS), BF16),
            pltpu.VMEM((EDGES, D), F32),
            pltpu.VMEM((EDGES, D), F32),
            pltpu.VMEM((EDGES, 1), F32),
            pltpu.VMEM((EDGES, D), BF16),
            pltpu.VMEM((EDGES, D), BF16),
            pltpu.VMEM((8, 128), F32),
            pltpu.VMEM((3, 8, 128), F32),
            pltpu.VMEM((8, 128), F32),
            pltpu.VMEM((NZ, 8, 128), F32),
            pltpu.VMEM((32, D), BF16),
            pltpu.VMEM((HALO, D), BF16),
            pltpu.VMEM((HALO, D), BF16),
            pltpu.VMEM((HALO, D), BF16),
            pltpu.VMEM((3, ROWS, D), BF16),
            pltpu.VMEM((3, ROWS, D), BF16),
            pltpu.VMEM((COARSE, D), BF16),
            pltpu.VMEM((7, 32, D), BF16),
            pltpu.VMEM((NZ, 8, 128), F32),
            pltpu.VMEM((NZ, 8, 128), F32),
            pltpu.VMEM((8, 128), F32),
            pltpu.VMEM((3, 8, 128), F32),
            pltpu.SemaphoreType.DMA((N_SEM,)),
            pltpu.SemaphoreType.DMA((N_SEM,)),
            pltpu.SemaphoreType.DMA((2,)),
        ],
        compiler_params=pltpu.CompilerParams(
            collective_id=0, has_side_effects=True, vmem_limit_bytes=50 * 2**20
        ),
    )(
        coarse, halo_count, node, edge, weights.reshape(7, 4, 2, 16, D), biases, gains, shifts,
        halo_send.reshape(1, HALO), esend.reshape(1, EDGES), erecv.reshape(1, EDGES), cot,
    )


def solution(mesh):
    rows = P(("dom", "feat"), None)
    flat = P(("dom", "feat"))
    return jax.shard_map(
        body,
        mesh=mesh,
        in_specs=(
            rows, rows, P(None, "feat", None), P(), P(), P(),
            P("dom", None, None), P("dom", None), P("dom", None), flat, flat, rows,
        ),
        out_specs=(rows, rows),
        check_vma=False,
    )
```

```python
import jax
import jax.numpy as jnp
from jax import lax
from jax.experimental import pallas as pl
from jax.experimental.pallas import tpu as pltpu
from jax.sharding import PartitionSpec as P

MESH = pl.DeviceIdType.MESH
F32, BF16 = jnp.float32, jnp.bfloat16
D = 512
ROWS = 256
EDGES = 768
BLOCK = 128
SLOTS = 384
PART = 1024
HALO = 256
COARSE = 256
TABLE = PART + HALO + COARSE
OFFSETS = (1, -1, 2, -2)
NZ, NY, NX = 16, 4, 4
GROUPS = ((0, 3), (3, 4))
EPS = 1e-05

COUNTS = dict(c1=3, w1=12, lat=3, c2=15, w2=12, halo=4, w3=4, c3=7, hb=4, rs=3, rc1=7, rc2=15, rc3=3)
BASE = {}
_total = 0
for _name, _n in COUNTS.items():
    BASE[_name] = _total
    _total += _n
N_SEM = _total


def dot(a, b):
    return jnp.dot(a, b, preferred_element_type=F32)


def dot_t(a, b):
    return lax.dot_general(a, b, (((1,), (1,)), ((), ())), preferred_element_type=F32)


def sigmoid(v):
    return 1.0 / (1.0 + jnp.exp(-v))


def onehot(mask):
    return jnp.where(mask, 1.0, 0.0).astype(BF16)


def iota(shape, dim):
    return lax.broadcasted_iota(jnp.int32, shape, dim)


def columns(row):
    wide = jnp.broadcast_to(row.astype(F32), (128, row.shape[1]))
    return wide.T.astype(jnp.int32)


def norm(values):
    centred = values - jnp.mean(values, axis=-1, keepdims=True)
    inv = lax.rsqrt(jnp.mean(centred * centred, axis=-1, keepdims=True) + EPS)
    return centred * inv, inv


def norm_back(scaled, normed, inv):
    return inv * (
        scaled
        - jnp.mean(scaled, axis=-1, keepdims=True)
        - normed * jnp.mean(scaled * normed, axis=-1, keepdims=True)
    )


def kernel(
    coarse_ref, count_ref, node_hbm, edge_hbm, wsh_ref, bias_hbm, gain_hbm, shift_hbm,
    halo_hbm, esend_hbm, erecv_hbm, cot_hbm,
    out_ref, grad_ref,
    node_ref, edge_ref, bias_ref, gain_ref, shift_ref, halo_ref, esend_ref, erecv_ref, cot_ref,
    lat, tab, w, sel, sel_t, hsel, own_part, rsel, rsel_t, hid, normed_e, inv_e, msg, hg,
    c1_src, c1_buf, c2_src, c2_buf, c3_src, halo_src, hb_src, hb_buf, part_src, rs_buf,
    rc1_src, rc1_buf, rc2_src, rc2_buf, rc3_src, rc3_buf,
    send_sem, recv_sem, local_sem, met_sem,
):
    dom, x = lax.axis_index("dom"), lax.axis_index("feat")
    z, y, c = dom // 8, (dom // 2) % 4, dom % 2
    yc = dom % 8
    zm = z % 4

    def at_x(d):
        return (dom, (x + d) % NX)

    def at_z(d):
        return (((z + d + NZ) % NZ) * 8 + yc, x)

    def at_y(d):
        return (z * 8 + ((y + d) % NY) * 2 + c, x)

    def at_yc(e):
        return (z * 8 + (yc + e) % 8, x)

    def at_dom(o):
        return ((dom + o + 128) % 128, x)

    other_core = (z * 8 + y * 2 + (1 - c), x)

    def copy(name, number, src, dst, device):
        at = BASE[name] + number
        return pltpu.make_async_remote_copy(
            src_ref=src, dst_ref=dst, send_sem=send_sem.at[at], recv_sem=recv_sem.at[at],
            device_id=device, device_id_type=MESH,
        )

    barrier = pltpu.get_barrier_semaphore()
    for d in (1, 2, 3):
        pl.semaphore_signal(barrier, inc=1, device_id=at_x(d), device_id_type=MESH)
    for e in range(1, 8):
        pl.semaphore_signal(barrier, inc=1, device_id=at_yc(e), device_id_type=MESH)
    for o in OFFSETS:
        pl.semaphore_signal(barrier, inc=1, device_id=at_dom(o), device_id_type=MESH)

    for d in (1, -1, 2, -2):
        pl.semaphore_signal(barrier, inc=1, device_id=at_z(d), device_id_type=MESH)

    fetches = {}
    pairs = dict(
        node=(node_hbm, node_ref), halo=(halo_hbm, halo_ref), esend=(esend_hbm, esend_ref),
        erecv=(erecv_hbm, erecv_ref), edge=(edge_hbm, edge_ref), cot=(cot_hbm, cot_ref),
        bias=(bias_hbm, bias_ref), gain=(gain_hbm, gain_ref), shift=(shift_hbm, shift_ref),
    )
    for number, (name, (source, target)) in enumerate(pairs.items()):
        fetches[name] = pltpu.make_async_copy(source, target, local_sem.at[2 + number])
        fetches[name].start()
    fetches["node"].wait()

    row8 = iota((8, ROWS), 0)
    wanted = jnp.where(row8 % 2 == 0, coarse_ref[0, 0], coarse_ref[0, 1]) - x * ROWS
    picked = dot(onehot(wanted == iota((8, ROWS), 1)), node_ref[...])
    quarter = iota((8, 128), 0) // 2
    tile = jnp.zeros((8, 128), F32)
    for j in range(4):
        tile = jnp.where(quarter == j, picked[:, 128 * j : 128 * j + 128], tile)
    c1_src[...] = tile

    own_rows = pl.ds(pl.multiple_of(x * ROWS, ROWS), ROWS)
    lat[own_rows, :] = node_ref[...]
    pl.semaphore_wait(barrier, 3 + 7 + 4 + 4)

    c1 = [copy("c1", d - 1, c1_src, c1_buf.at[d - 1], at_x(d)) for d in (1, 2, 3)]
    for one in c1:
        one.start()
    pieces = ((y, 0), (zm, 1))
    w1 = {}
    for g, (first, count) in enumerate(GROUPS):
        mats = pl.ds(first, count)
        for t, (j, _) in enumerate(pieces):
            cols = pl.ds(256 * t, 256)
            for d in (2, 1, 3):
                w1[g, t, d] = copy(
                    "w1", (g * 2 + t) * 3 + d - 1,
                    wsh_ref.at[mats, j, c, :, cols], w.at[mats, NX - d, j, c, :, cols], at_x(d),
                )
                w1[g, t, d].start()
    lat_copies = [copy("lat", d - 1, node_hbm, lat.at[own_rows, :], at_x(d)) for d in (2, 1, 3)]
    for one in lat_copies:
        one.start()
    for d in (2, -2):
        pl.semaphore_signal(met_sem.at[0], inc=1, device_id=at_z(d), device_id_type=MESH)
    own = pltpu.make_async_copy(wsh_ref, w.at[:, 0], local_sem.at[0])
    own.start()

    fetches["halo"].wait()
    halo_row = jnp.concatenate([halo_ref[0, k : k + 1, :] for k in range(4)], axis=1)
    lane = iota((1, HALO), 1)
    live = count_ref[0, 0]
    for k in (1, 2, 3):
        live = jnp.where(lane // 64 == k, count_ref[0, k], live)
    halo_row = jnp.where(lane % 64 < live, halo_row, -1)
    halo_col = columns(halo_row)

    pl.semaphore_wait(met_sem.at[0], 2)
    for d in (4, -4):
        pl.semaphore_signal(met_sem.at[1], inc=1, device_id=at_z(d), device_id_type=MESH)

    for one in c1:
        one.wait_recv()
    pl.semaphore_wait(met_sem.at[1], 2)
    total = c1_src[...] + c1_buf[0] + c1_buf[1] + c1_buf[2]
    c2_src[...] = total
    c2_buf[z] = total

    def c2(d):
        at = BASE["c2"] + d - 1
        return pltpu.make_async_remote_copy(
            src_ref=c2_src, dst_ref=c2_buf.at[z],
            send_sem=send_sem.at[at], recv_sem=recv_sem.at[at],
            device_id=at_z(d), device_id_type=MESH,
        )

    order = [8]
    for i in range(1, 8):
        order += [8 - i, 8 + i]
    for d in order:
        c2(d).start()

    fetches["esend"].wait()
    index = esend_ref[...].reshape(1, EDGES)
    m = index - (PART + HALO)
    index = jnp.where(
        m >= 0, PART + HALO + ((m >> 1) & 7) * 32 + (m >> 4) * 2 + (m & 1), index
    )

    def w2_start(g):
        first, count = GROUPS[g]
        mats = pl.ds(first, count)
        started = []
        for t, (j, _) in enumerate(pieces):
            cols = pl.ds(256 * t, 256)
            for d in (1, 2, 3):
                w1[g, t, d].wait_recv()
            for d in (2, 1, 3):
                step = d if d < 3 else -1
                target = at_y(d) if t == 0 else at_z(step)
                part = w.at[mats, pl.ds(1, 3), j, c, :, cols]
                one = copy("w2", (g * 2 + t) * 3 + d - 1, part, part, target)
                one.start()
                started.append(one)
        return started

    def w3_start(g, arrived):
        first, count = GROUPS[g]
        mats = pl.ds(first, count)
        started = []
        for t in range(2):
            for one in arrived[3 * t : 3 * t + 3]:
                one.wait_recv()
            part = w.at[mats, pl.ds(1, 3), :, c, :, pl.ds(256 * t, 256)]
            one = copy("w3", g * 2 + t, part, part, other_core)
            one.start()
            started.append(one)
        return started

    w2a = w2_start(0)
    index_col = columns(index)
    for j in range(TABLE // 128):
        sel[:, 128 * j : 128 * j + 128] = onehot(index_col == iota((EDGES, 128), 1) + 128 * j)
    w2b = w2_start(1)
    fetches["erecv"].wait()
    recv_row = erecv_ref[...].reshape(1, EDGES)
    recv_col = columns(recv_row)
    rsel[...] = onehot(recv_col == iota((EDGES, 128), 1))
    for b in range(2):
        rsel_t[b] = onehot(
            iota((BLOCK, SLOTS), 0) == recv_row[:, SLOTS * b : SLOTS * b + SLOTS]
        )

    for j in range(PART // 128):
        hsel[:, 128 * j : 128 * j + 128] = onehot(halo_col == iota((HALO, 128), 1) + 128 * j)
    for j in range(TABLE // 128):
        sel_t[128 * j : 128 * j + 128, :] = onehot(iota((128, EDGES), 0) + 128 * j == index)
    for d in order:
        c2(d).wait_recv()
    flat = c2_buf[...].reshape(NZ * 8, 128).astype(BF16)
    parts = []
    for j in range(4):
        row = iota((32, 128), 0)
        parts.append(dot(onehot((row // 2) * 8 + 2 * j + row % 2 == iota((32, 128), 1)), flat))
    own_coarse = jnp.concatenate(parts, axis=1).astype(BF16)
    c3_src[...] = own_coarse
    coarse_rows = pl.ds(pl.multiple_of(PART + HALO + yc * 32, 32), 32)
    lat[coarse_rows, :] = own_coarse
    c3 = [copy("c3", e - 1, c3_src, lat.at[coarse_rows, :], at_yc(e)) for e in range(1, 8)]
    for one in c3:
        one.start()
    w3a = w3_start(0, w2a)
    for one in lat_copies:
        one.wait_recv()
    halo_src[...] = dot(hsel[...], lat[:PART, :]).astype(BF16)
    halo_copies = []
    for k in range(4):
        one = copy(
            "halo", k, halo_src.at[pl.ds(64 * k, 64)], lat.at[pl.ds(PART + 64 * k, 64)], at_dom(OFFSETS[k])
        )
        one.start()
        halo_copies.append(one)

    w3b = w3_start(1, w2b)

    def weight(i):
        return jnp.concatenate(
            [w[i, (k - x + NX) % NX].reshape(D // NX, D) for k in range(NX)], axis=0
        )

    own.wait()

    for name in ("edge", "cot", "bias", "gain", "shift"):
        fetches[name].wait()
    for one in w3a:
        one.wait_recv()
    w_e, w_s, w_r = weight(0), weight(1), weight(2)
    recv_proj = dot(node_ref[...], w_r).astype(BF16)
    for j in range(4):
        rows = slice(256 * j, 256 * j + 256)
        tab[rows, :] = dot(lat[rows, :], w_s).astype(BF16)
    for b in range(2):
        rows = slice(SLOTS * b, SLOTS * b + SLOTS)
        hid[rows, :] = (
            dot(edge_ref[rows, :], w_e)
            + dot(rsel[rows, :], recv_proj[BLOCK * b : BLOCK * b + BLOCK])
            + dot(sel[rows, :PART], tab[:PART, :])
            + bias_ref[0:1, :]
        )
    for one in c3:
        one.wait_recv()
    rows = slice(PART + HALO, TABLE)
    tab[rows, :] = dot(lat[rows, :], w_s).astype(BF16)
    hid[...] += dot(sel[:, PART + HALO :], tab[rows, :])
    for one in halo_copies:
        one.wait_recv()
    rows = slice(PART, PART + HALO)
    tab[rows, :] = dot(lat[rows, :], w_s).astype(BF16)

    for one in w3b:
        one.wait_recv()
    aggregate = []
    for b in range(2):
        rows = slice(SLOTS * b, SLOTS * b + SLOTS)
        h = hid[rows, :] + dot(sel[rows, PART : PART + HALO], tab[PART : PART + HALO, :])
        hid[rows, :] = h
        act = (h * sigmoid(h)).astype(BF16)
        normed, inv = norm(dot(act, weight(3)) + bias_ref[1:2, :])
        normed_e[rows, :] = normed
        inv_e[rows, :] = inv
        msg[rows, :] = (normed * gain_ref[0:1, :] + shift_ref[0:1, :]).astype(BF16)
        aggregate.append(dot(rsel_t[b], msg[rows, :]).astype(BF16))
    aggregate = jnp.concatenate(aggregate, axis=0)
    node = node_ref[...]
    node_in = dot(node, weight(4)) + dot(aggregate, weight(5)) + bias_ref[2:3, :]
    s = sigmoid(node_in)
    slope = s * (1.0 + node_in * (1.0 - s))
    normed, inv = norm(dot((node_in * s).astype(BF16), weight(6)) + bias_ref[3:4, :])
    out_ref[...] = (
        node.astype(F32) + (normed * gain_ref[1:2, :] + shift_ref[1:2, :])
    ).astype(BF16)
    cot = cot_ref[...].astype(F32)
    node_back = norm_back(cot * gain_ref[1:2, :], normed, inv).astype(BF16)
    node_in_grad = (dot_t(node_back, weight(6)) * slope).astype(BF16)
    agg_grad = dot_t(node_in_grad, weight(5)).astype(BF16)
    for b in range(2):
        rows = slice(SLOTS * b, SLOTS * b + SLOTS)
        back = dot(rsel[rows, :], agg_grad[BLOCK * b : BLOCK * b + BLOCK])
        edge_back = norm_back(back * gain_ref[0:1, :], normed_e[rows, :], inv_e[rows, :]).astype(BF16)
        h = hid[rows, :]
        s = sigmoid(h)
        hg[rows, :] = (dot_t(edge_back, weight(3)) * (s * (1.0 + h * (1.0 - s)))).astype(BF16)

    hb_src[...] = dot(sel_t[PART : PART + HALO, :], hg[...]).astype(BF16)
    hb = []
    for k in range(4):
        part = pl.ds(64 * k, 64)
        hb.append(copy("hb", k, hb_src.at[part], hb_buf.at[part], at_dom(-OFFSETS[k])))
        hb[-1].start()
    rc1_src[...] = dot(sel_t[PART + HALO :, :], hg[...]).astype(BF16)
    rc1 = [
        copy(
            "rc1", e - 1,
            rc1_src.at[pl.ds(pl.multiple_of((yc + e) % 8 * 32, 32), 32)], rc1_buf.at[e - 1], at_yc(e),
        )
        for e in range(1, 8)
    ]
    for one in rc1:
        one.start()

    starts = [pl.multiple_of(((x + d) % NX) * ROWS, ROWS) for d in range(NX)]
    for d in (2, 1, 3, 0):
        own_part[d] = dot(sel_t[pl.ds(starts[d], ROWS), :], hg[...])
    recv_grad = [
        dot(rsel_t[b], hg[SLOTS * b : SLOTS * b + SLOTS, :]).astype(BF16) for b in range(2)
    ]
    grad_ref[...] = (
        cot_ref[...].astype(F32)
        + dot_t(node_in_grad, weight(4))
        + dot_t(jnp.concatenate(recv_grad, axis=0), weight(2))
    )

    for one in hb:
        one.wait_recv()
    rs = []
    for d in (2, 1, 3):
        place = onehot(iota((ROWS, HALO), 0) + starts[d] == halo_row)
        part_src[d - 1] = (own_part[d] + dot(place, hb_buf[...])).astype(BF16)
        rs.append(copy("rs", d - 1, part_src.at[d - 1], rs_buf.at[d - 1], at_x(d)))
        rs[-1].start()

    for one in rc1:
        one.wait_recv()
    gathered = rc1_src[pl.ds(pl.multiple_of(yc * 32, 32), 32), :].astype(F32)
    for e in range(7):
        gathered += rc1_buf[e].astype(F32)
    gathered = gathered.astype(BF16)
    spread = jnp.zeros((NZ * 8, 128), F32)
    for j in range(4):
        row, col = iota((NZ * 8, 32), 0), iota((NZ * 8, 32), 1)
        place = (row // 8 == col // 2) & (row % 8 == 2 * j + col % 2)
        spread += dot(onehot(place), gathered[:, 128 * j : 128 * j + 128])
    rc2_src[...] = spread.reshape(NZ, 8, 128)
    rc2_buf[z] = rc2_src[z]

    def rc2(d):
        at = BASE["rc2"] + d - 1
        return pltpu.make_async_remote_copy(
            src_ref=rc2_src.at[(z + d) % NZ], dst_ref=rc2_buf.at[z],
            send_sem=send_sem.at[at], recv_sem=recv_sem.at[at],
            device_id=at_z(d), device_id_type=MESH,
        )

    for d in order:
        rc2(d).start()

    place = onehot(iota((ROWS, HALO), 0) + starts[0] == halo_row)
    own_part[0] += dot(place, hb_buf[...])

    for d in order:
        rc2(d).wait_recv()
    tile = jnp.sum(rc2_buf[...], axis=0)
    rc3_src[...] = tile
    rc3 = [copy("rc3", d - 1, rc3_src, rc3_buf.at[d - 1], at_x(d)) for d in (1, 2, 3)]
    for one in rc3:
        one.start()
    for one in rc3:
        one.wait_recv()
    tile = rc3_src[...] + rc3_buf[0] + rc3_buf[1] + rc3_buf[2]
    for one in rs:
        one.wait_recv()
    value = own_part[0]
    for d in range(3):
        value += rs_buf[d].astype(F32)
    for i in range(2):
        line = jnp.concatenate([tile[2 * j + i : 2 * j + i + 1, :] for j in range(4)], axis=1)
        here = iota((ROWS, D), 0) + x * ROWS == coarse_ref[0, i]
        value += jnp.where(here, line, 0.0)
    grad_ref[...] += dot_t(value.astype(BF16), weight(1))

    for one in c1 + list(w1.values()) + lat_copies + w2a + w2b + w3a + w3b:
        one.wait_send()
    for one in halo_copies + c3 + rc1 + hb + rs + rc3:
        one.wait_send()
    for d in order:
        c2(d).wait_send()
        rc2(d).wait_send()


def body(node, edge, weights, biases, gains, shifts, halo_send, halo_count, coarse, esend, erecv, cot):
    vmem = pl.BlockSpec(memory_space=pltpu.VMEM)
    smem = pl.BlockSpec(memory_space=pltpu.SMEM)
    return pl.pallas_call(
        kernel,
        name="layer",
        out_shape=(
            jax.ShapeDtypeStruct((ROWS, D), BF16),
            jax.ShapeDtypeStruct((ROWS, D), F32),
        ),
        in_specs=[smem, smem] + [pl.BlockSpec(memory_space=pl.ANY)] * 10,
        out_specs=(vmem, vmem),
        scratch_shapes=[
            pltpu.VMEM((ROWS, D), BF16),
            pltpu.VMEM((EDGES, D), BF16),
            pltpu.VMEM((4, D), F32),
            pltpu.VMEM((2, D), F32),
            pltpu.VMEM((2, D), F32),
            pltpu.VMEM((1, 4, 64), jnp.int32),
            pltpu.VMEM((EDGES,), jnp.int32),
            pltpu.VMEM((EDGES,), jnp.int32),
            pltpu.VMEM((ROWS, D), BF16),
            pltpu.VMEM((TABLE, D), BF16),
            pltpu.VMEM((TABLE, D), BF16),
            pltpu.VMEM((7, NX, 4, 2, 16, D), BF16),
            pltpu.VMEM((EDGES, TABLE), BF16),
            pltpu.VMEM((TABLE, EDGES), BF16),
            pltpu.VMEM((HALO, PART), BF16),
            pltpu.VMEM((NX, ROWS, D), F32),
            pltpu.VMEM((EDGES, BLOCK), BF16),
            pltpu.VMEM((2, BLOCK, SLOTS), BF16),
            pltpu.VMEM((EDGES, D), F32),
            pltpu.VMEM((EDGES, D), F32),
            pltpu.VMEM((EDGES, 1), F32),
            pltpu.VMEM((EDGES, D), BF16),
            pltpu.VMEM((EDGES, D), BF16),
            pltpu.VMEM((8, 128), F32),
            pltpu.VMEM((3, 8, 128), F32),
            pltpu.VMEM((8, 128), F32),
            pltpu.VMEM((NZ, 8, 128), F32),
            pltpu.VMEM((32, D), BF16),
            pltpu.VMEM((HALO, D), BF16),
            pltpu.VMEM((HALO, D), BF16),
            pltpu.VMEM((HALO, D), BF16),
            pltpu.VMEM((3, ROWS, D), BF16),
            pltpu.VMEM((3, ROWS, D), BF16),
            pltpu.VMEM((COARSE, D), BF16),
            pltpu.VMEM((7, 32, D), BF16),
            pltpu.VMEM((NZ, 8, 128), F32),
            pltpu.VMEM((NZ, 8, 128), F32),
            pltpu.VMEM((8, 128), F32),
            pltpu.VMEM((3, 8, 128), F32),
            pltpu.SemaphoreType.DMA((N_SEM,)),
            pltpu.SemaphoreType.DMA((N_SEM,)),
            pltpu.SemaphoreType.DMA((11,)),
            pltpu.SemaphoreType.REGULAR((2,)),
        ],
        compiler_params=pltpu.CompilerParams(
            collective_id=0, has_side_effects=True, vmem_limit_bytes=60 * 2**20
        ),
    )(
        coarse, halo_count, node, edge, weights.reshape(7, 4, 2, 16, D), biases, gains, shifts,
        halo_send, esend, erecv, cot,
    )


def solution(mesh):
    rows = P(("dom", "feat"), None)
    flat = P(("dom", "feat"))
    return jax.shard_map(
        body,
        mesh=mesh,
        in_specs=(
            rows, rows, P(None, "feat", None), P(), P(), P(),
            P("dom", None, None), P("dom", None), P("dom", None), flat, flat, rows,
        ),
        out_specs=(rows, rows),
        check_vma=False,
    )
```

```python
import jax
import jax.numpy as jnp
from jax import lax
from jax.experimental import pallas as pl
from jax.experimental.pallas import tpu as pltpu
from jax.sharding import PartitionSpec as P

MESH = pl.DeviceIdType.MESH
F32, BF16 = jnp.float32, jnp.bfloat16
D = 512
ROWS = 256
EDGES = 768
BLOCK = 128
SLOTS = 384
PART = 1024
HALO = 256
COARSE = 256
TABLE = PART + HALO + COARSE
OFFSETS = (1, -1, 2, -2)
NZ, NY, NX = 16, 4, 4
GROUPS = ((0, 3), (3, 4))
EPS = 1e-05

COUNTS = dict(c1=3, w1=12, lat=3, c2=15, w2=12, halo=4, w3=4, c3=3, c3b=1, hb=4, rs=6, rca=1, rc1=3, rc2=15, rc3=3)
BASE = {}
_total = 0
for _name, _n in COUNTS.items():
    BASE[_name] = _total
    _total += _n
N_SEM = _total


def dot(a, b):
    return jnp.dot(a, b, preferred_element_type=F32)


def dot_t(a, b):
    return lax.dot_general(a, b, (((1,), (1,)), ((), ())), preferred_element_type=F32)


def sigmoid(v):
    return 1.0 / (1.0 + jnp.exp(-v))


def onehot(mask):
    return jnp.where(mask, 1.0, 0.0).astype(BF16)


def iota(shape, dim):
    return lax.broadcasted_iota(jnp.int32, shape, dim)


def columns(row):
    wide = jnp.broadcast_to(row.astype(F32), (128, row.shape[1]))
    return wide.T.astype(jnp.int32)


def norm(values):
    centred = values - jnp.mean(values, axis=-1, keepdims=True)
    inv = lax.rsqrt(jnp.mean(centred * centred, axis=-1, keepdims=True) + EPS)
    return centred * inv, inv


def norm_back(scaled, normed, inv):
    return inv * (
        scaled
        - jnp.mean(scaled, axis=-1, keepdims=True)
        - normed * jnp.mean(scaled * normed, axis=-1, keepdims=True)
    )


def kernel(
    coarse_ref, count_ref, node_hbm, edge_hbm, wsh_ref, bias_hbm, gain_hbm, shift_hbm,
    halo_hbm, esend_hbm, erecv_hbm, cot_hbm,
    out_ref, grad_ref,
    node_ref, edge_ref, bias_ref, gain_ref, shift_ref, halo_ref, esend_ref, erecv_ref, cot_ref,
    lat, tab, w, sel, sel_t, hsel, own_part, rsel, rsel_t, hid, normed_e, inv_e, msg, hg,
    c1_src, c1_buf, c2_src, c2_buf, c3_src, halo_src, hb_src, hb_buf, part_src, rs_buf, far_buf, ctab, rca_buf, pair_sum, pair_src,
    rc1_src, rc1_buf, rc2_src, rc2_buf, rc3_src, rc3_buf,
    send_sem, recv_sem, local_sem, met_sem,
):
    dom, x = lax.axis_index("dom"), lax.axis_index("feat")
    z, y, c = dom // 8, (dom // 2) % 4, dom % 2
    yc = dom % 8
    zm = z % 4

    def at_x(d):
        return (dom, (x + d) % NX)

    def at_z(d):
        return (((z + d + NZ) % NZ) * 8 + yc, x)

    def at_y(d):
        return (z * 8 + ((y + d) % NY) * 2 + c, x)

    def at_yc(e):
        return (z * 8 + (yc + e) % 8, x)

    def at_dom(o):
        return ((dom + o + 128) % 128, x)

    other_core = (z * 8 + y * 2 + (1 - c), x)

    def copy(name, number, src, dst, device):
        at = BASE[name] + number
        return pltpu.make_async_remote_copy(
            src_ref=src, dst_ref=dst, send_sem=send_sem.at[at], recv_sem=recv_sem.at[at],
            device_id=device, device_id_type=MESH,
        )

    barrier = pltpu.get_barrier_semaphore()
    for d in (1, 2, 3):
        pl.semaphore_signal(barrier, inc=1, device_id=at_x(d), device_id_type=MESH)
    for e in range(1, 8):
        pl.semaphore_signal(barrier, inc=1, device_id=at_yc(e), device_id_type=MESH)
    for o in OFFSETS:
        pl.semaphore_signal(barrier, inc=1, device_id=at_dom(o), device_id_type=MESH)

    for d in (1, -1, 2, -2):
        pl.semaphore_signal(barrier, inc=1, device_id=at_z(d), device_id_type=MESH)

    fetches = {}
    pairs = dict(
        node=(node_hbm, node_ref), halo=(halo_hbm, halo_ref), esend=(esend_hbm, esend_ref),
        erecv=(erecv_hbm, erecv_ref), edge=(edge_hbm, edge_ref), cot=(cot_hbm, cot_ref),
        bias=(bias_hbm, bias_ref), gain=(gain_hbm, gain_ref), shift=(shift_hbm, shift_ref),
    )
    for number, (name, (source, target)) in enumerate(pairs.items()):
        fetches[name] = pltpu.make_async_copy(source, target, local_sem.at[2 + number])
        fetches[name].start()
    fetches["node"].wait()

    row8 = iota((8, ROWS), 0)
    wanted = jnp.where(row8 % 2 == 0, coarse_ref[0, 0], coarse_ref[0, 1]) - x * ROWS
    picked = dot(onehot(wanted == iota((8, ROWS), 1)), node_ref[...])
    quarter = iota((8, 128), 0) // 2
    tile = jnp.zeros((8, 128), F32)
    for j in range(4):
        tile = jnp.where(quarter == j, picked[:, 128 * j : 128 * j + 128], tile)
    c1_src[...] = tile

    own_rows = pl.ds(pl.multiple_of(x * ROWS, ROWS), ROWS)
    lat[own_rows, :] = node_ref[...]
    pl.semaphore_wait(barrier, 3 + 7 + 4 + 4)

    c1 = [copy("c1", d - 1, c1_src, c1_buf.at[d - 1], at_x(d)) for d in (1, 2, 3)]
    for one in c1:
        one.start()
    pieces = ((y, 0), (zm, 1))
    w1 = {}
    for g, (first, count) in enumerate(GROUPS):
        mats = pl.ds(first, count)
        for t, (j, _) in enumerate(pieces):
            cols = pl.ds(256 * t, 256)
            for d in (2, 1, 3):
                w1[g, t, d] = copy(
                    "w1", (g * 2 + t) * 3 + d - 1,
                    wsh_ref.at[mats, j, c, :, cols], w.at[mats, NX - d, j, c, :, cols], at_x(d),
                )
                w1[g, t, d].start()
    lat_copies = [copy("lat", d - 1, node_hbm, lat.at[own_rows, :], at_x(d)) for d in (2, 1, 3)]
    for one in lat_copies:
        one.start()
    for d in (2, -2):
        pl.semaphore_signal(met_sem.at[0], inc=1, device_id=at_z(d), device_id_type=MESH)
    own = pltpu.make_async_copy(wsh_ref, w.at[:, 0], local_sem.at[0])
    own.start()

    fetches["halo"].wait()
    halo_row = jnp.concatenate([halo_ref[0, k : k + 1, :] for k in range(4)], axis=1)
    lane = iota((1, HALO), 1)
    live = count_ref[0, 0]
    for k in (1, 2, 3):
        live = jnp.where(lane // 64 == k, count_ref[0, k], live)
    halo_row = jnp.where(lane % 64 < live, halo_row, -1)
    halo_col = columns(halo_row)

    pl.semaphore_wait(met_sem.at[0], 2)
    for d in (4, -4):
        pl.semaphore_signal(met_sem.at[1], inc=1, device_id=at_z(d), device_id_type=MESH)

    for one in c1:
        one.wait_recv()
    pl.semaphore_wait(met_sem.at[1], 2)
    total = c1_src[...] + c1_buf[0] + c1_buf[1] + c1_buf[2]
    c2_src[...] = total
    c2_buf[z] = total

    def c2(d):
        at = BASE["c2"] + d - 1
        return pltpu.make_async_remote_copy(
            src_ref=c2_src, dst_ref=c2_buf.at[z],
            send_sem=send_sem.at[at], recv_sem=recv_sem.at[at],
            device_id=at_z(d), device_id_type=MESH,
        )

    order = [8]
    for i in range(1, 8):
        order += [8 - i, 8 + i]
    for d in order:
        c2(d).start()

    fetches["esend"].wait()
    index = esend_ref[...].reshape(1, EDGES)
    m = index - (PART + HALO)
    index = jnp.where(
        m >= 0, PART + HALO + ((m >> 1) & 7) * 32 + (m >> 4) * 2 + (m & 1), index
    )

    def w2_start(g):
        first, count = GROUPS[g]
        mats = pl.ds(first, count)
        started = []
        for t, (j, _) in enumerate(pieces):
            cols = pl.ds(256 * t, 256)
            for d in (1, 2, 3):
                w1[g, t, d].wait_recv()
            for d in (2, 1, 3):
                step = d if d < 3 else -1
                target = at_y(d) if t == 0 else at_z(step)
                part = w.at[mats, pl.ds(1, 3), j, c, :, cols]
                one = copy("w2", (g * 2 + t) * 3 + d - 1, part, part, target)
                one.start()
                started.append(one)
        return started

    def w3_start(g, arrived):
        first, count = GROUPS[g]
        mats = pl.ds(first, count)
        started = []
        for t in range(2):
            for one in arrived[3 * t : 3 * t + 3]:
                one.wait_recv()
            part = w.at[mats, pl.ds(1, 3), :, c, :, pl.ds(256 * t, 256)]
            one = copy("w3", g * 2 + t, part, part, other_core)
            one.start()
            started.append(one)
        return started

    w2a = w2_start(0)
    index_col = columns(index)
    for j in range(TABLE // 128):
        sel[:, 128 * j : 128 * j + 128] = onehot(index_col == iota((EDGES, 128), 1) + 128 * j)
    w2b = w2_start(1)
    fetches["erecv"].wait()
    recv_row = erecv_ref[...].reshape(1, EDGES)
    recv_col = columns(recv_row)
    rsel[...] = onehot(recv_col == iota((EDGES, 128), 1))
    for b in range(2):
        rsel_t[b] = onehot(
            iota((BLOCK, SLOTS), 0) == recv_row[:, SLOTS * b : SLOTS * b + SLOTS]
        )

    for j in range(PART // 128):
        hsel[:, 128 * j : 128 * j + 128] = onehot(halo_col == iota((HALO, 128), 1) + 128 * j)
    for j in range(TABLE // 128):
        sel_t[128 * j : 128 * j + 128, :] = onehot(iota((128, EDGES), 0) + 128 * j == index)
    for d in order:
        c2(d).wait_recv()
    flat = c2_buf[...].reshape(NZ * 8, 128).astype(BF16)
    parts = []
    for j in range(4):
        row = iota((32, 128), 0)
        parts.append(dot(onehot((row // 2) * 8 + 2 * j + row % 2 == iota((32, 128), 1)), flat))
    own_coarse = jnp.concatenate(parts, axis=1).astype(BF16)
    c3_src[...] = own_coarse
    ctab[y, c] = own_coarse
    c3 = [copy("c3", d - 1, c3_src, ctab.at[y, c], at_y(d)) for d in (2, 1, 3)]
    for one in c3:
        one.start()
    w3a = w3_start(0, w2a)
    for one in lat_copies:
        one.wait_recv()
    halo_src[...] = dot(hsel[...], lat[:PART, :]).astype(BF16)
    halo_copies = []
    for k in range(4):
        one = copy(
            "halo", k, halo_src.at[pl.ds(64 * k, 64)], lat.at[pl.ds(PART + 64 * k, 64)], at_dom(OFFSETS[k])
        )
        one.start()
        halo_copies.append(one)

    for one in c3:
        one.wait_recv()
    c3b = [copy("c3b", 0, ctab.at[:, c], ctab.at[:, c], other_core)]
    c3b[0].start()
    w3b = w3_start(1, w2b)

    def weight(i):
        return jnp.concatenate(
            [w[i, (k - x + NX) % NX].reshape(D // NX, D) for k in range(NX)], axis=0
        )

    own.wait()

    for name in ("edge", "cot", "bias", "gain", "shift"):
        fetches[name].wait()
    for one in w3a:
        one.wait_recv()
    w_e, w_s, w_r = weight(0), weight(1), weight(2)
    recv_proj = dot(node_ref[...], w_r).astype(BF16)
    for j in range(4):
        rows = slice(256 * j, 256 * j + 256)
        tab[rows, :] = dot(lat[rows, :], w_s).astype(BF16)
    for b in range(2):
        rows = slice(SLOTS * b, SLOTS * b + SLOTS)
        hid[rows, :] = (
            dot(edge_ref[rows, :], w_e)
            + dot(rsel[rows, :], recv_proj[BLOCK * b : BLOCK * b + BLOCK])
            + dot(sel[rows, :PART], tab[:PART, :])
            + bias_ref[0:1, :]
        )
    for one in c3b:
        one.wait_recv()
    rows = slice(PART + HALO, TABLE)
    tab[rows, :] = dot(ctab[...].reshape(COARSE, D), w_s).astype(BF16)
    hid[...] += dot(sel[:, PART + HALO :], tab[rows, :])
    for one in halo_copies:
        one.wait_recv()
    rows = slice(PART, PART + HALO)
    tab[rows, :] = dot(lat[rows, :], w_s).astype(BF16)

    for one in w3b:
        one.wait_recv()
    aggregate = []
    for b in range(2):
        rows = slice(SLOTS * b, SLOTS * b + SLOTS)
        h = hid[rows, :] + dot(sel[rows, PART : PART + HALO], tab[PART : PART + HALO, :])
        hid[rows, :] = h
        act = (h * sigmoid(h)).astype(BF16)
        normed, inv = norm(dot(act, weight(3)) + bias_ref[1:2, :])
        normed_e[rows, :] = normed
        inv_e[rows, :] = inv
        msg[rows, :] = (normed * gain_ref[0:1, :] + shift_ref[0:1, :]).astype(BF16)
        aggregate.append(dot(rsel_t[b], msg[rows, :]).astype(BF16))
    aggregate = jnp.concatenate(aggregate, axis=0)
    node = node_ref[...]
    node_in = dot(node, weight(4)) + dot(aggregate, weight(5)) + bias_ref[2:3, :]
    s = sigmoid(node_in)
    slope = s * (1.0 + node_in * (1.0 - s))
    normed, inv = norm(dot((node_in * s).astype(BF16), weight(6)) + bias_ref[3:4, :])
    out_ref[...] = (
        node.astype(F32) + (normed * gain_ref[1:2, :] + shift_ref[1:2, :])
    ).astype(BF16)
    cot = cot_ref[...].astype(F32)
    node_back = norm_back(cot * gain_ref[1:2, :], normed, inv).astype(BF16)
    node_in_grad = (dot_t(node_back, weight(6)) * slope).astype(BF16)
    agg_grad = dot_t(node_in_grad, weight(5)).astype(BF16)
    for b in range(2):
        rows = slice(SLOTS * b, SLOTS * b + SLOTS)
        back = dot(rsel[rows, :], agg_grad[BLOCK * b : BLOCK * b + BLOCK])
        edge_back = norm_back(back * gain_ref[0:1, :], normed_e[rows, :], inv_e[rows, :]).astype(BF16)
        h = hid[rows, :]
        s = sigmoid(h)
        hg[rows, :] = (dot_t(edge_back, weight(3)) * (s * (1.0 + h * (1.0 - s)))).astype(BF16)

    hb_src[...] = dot(sel_t[PART : PART + HALO, :], hg[...]).astype(BF16)
    hb = []
    for k in range(4):
        part = pl.ds(64 * k, 64)
        hb.append(copy("hb", k, hb_src.at[part], hb_buf.at[part], at_dom(-OFFSETS[k])))
        hb[-1].start()
    rc1_src[...] = dot(sel_t[PART + HALO :, :], hg[...]).astype(BF16).reshape(4, 2, 32, D)
    rca = [copy("rca", 0, rc1_src.at[:, 1 - c], rca_buf, other_core)]
    rca[0].start()

    starts = [pl.multiple_of(((x + d) % NX) * ROWS, ROWS) for d in range(NX)]
    for d in (2, 1, 3, 0):
        own_part[d] = dot(sel_t[pl.ds(starts[d], ROWS), :], hg[...])
    for one in rca:
        one.wait_recv()
    pair_sum[...] = rc1_src[:, c].astype(F32) + rca_buf[...].astype(F32)
    pair_src[...] = pair_sum[...].astype(BF16)
    rc1 = [copy("rc1", d - 1, pair_src.at[(y + d) % NY], rc1_buf.at[d - 1], at_y(d)) for d in (2, 1, 3)]
    for one in rc1:
        one.start()
    recv_grad = [
        dot(rsel_t[b], hg[SLOTS * b : SLOTS * b + SLOTS, :]).astype(BF16) for b in range(2)
    ]
    grad_ref[...] = (
        cot_ref[...].astype(F32)
        + dot_t(node_in_grad, weight(4))
        + dot_t(jnp.concatenate(recv_grad, axis=0), weight(2))
    )

    for one in hb:
        one.wait_recv()
    half = ROWS // 2

    def with_halo(d):
        place = onehot(iota((ROWS, HALO), 0) + starts[d] == halo_row)
        return own_part[d] + dot(place, hb_buf[...])

    low, high = pl.ds(0, half), pl.ds(half, half)

    def rs_send(number, source, target, d):
        one = copy("rs", number, source, target, at_x(d))
        one.start()
        return one

    part_src[2] = with_halo(2).astype(BF16)
    rs_far = [
        rs_send(0, part_src.at[2, low], far_buf.at[0], 1),
        rs_send(1, part_src.at[2, high], far_buf.at[1], 3),
    ]
    next_sum, last_sum = with_halo(1), with_halo(3)
    own_part[1], own_part[3] = next_sum, last_sum
    part_src[0, high] = next_sum[half:].astype(BF16)
    part_src[1, low] = last_sum[:half].astype(BF16)
    rs = [
        rs_send(2, part_src.at[0, high], rs_buf.at[0, high], 1),
        rs_send(3, part_src.at[1, low], rs_buf.at[1, low], 3),
    ]

    for one in rc1:
        one.wait_recv()
    gathered = pair_sum[y]
    for e in range(3):
        gathered += rc1_buf[e].astype(F32)
    gathered = gathered.astype(BF16)
    spread = jnp.zeros((NZ * 8, 128), F32)
    for j in range(4):
        row, col = iota((NZ * 8, 32), 0), iota((NZ * 8, 32), 1)
        place = (row // 8 == col // 2) & (row % 8 == 2 * j + col % 2)
        spread += dot(onehot(place), gathered[:, 128 * j : 128 * j + 128])
    rc2_src[...] = spread.reshape(NZ, 8, 128)
    rc2_buf[z] = rc2_src[z]

    def rc2(d):
        at = BASE["rc2"] + d - 1
        return pltpu.make_async_remote_copy(
            src_ref=rc2_src.at[(z + d) % NZ], dst_ref=rc2_buf.at[z],
            send_sem=send_sem.at[at], recv_sem=recv_sem.at[at],
            device_id=at_z(d), device_id_type=MESH,
        )

    for d in order:
        rc2(d).start()

    own_part[0] = with_halo(0)
    for one in rs_far:
        one.wait_recv()
    part_src[0, low] = (own_part[1, low] + far_buf[0].astype(F32)).astype(BF16)
    rs.append(rs_send(4, part_src.at[0, low], rs_buf.at[0, low], 1))
    part_src[1, high] = (own_part[3, high] + far_buf[1].astype(F32)).astype(BF16)
    rs.append(rs_send(5, part_src.at[1, high], rs_buf.at[1, high], 3))

    for d in order:
        rc2(d).wait_recv()
    tile = jnp.sum(rc2_buf[...], axis=0)
    rc3_src[...] = tile
    rc3 = [copy("rc3", d - 1, rc3_src, rc3_buf.at[d - 1], at_x(d)) for d in (1, 2, 3)]
    for one in rc3:
        one.start()
    for one in rc3:
        one.wait_recv()
    tile = rc3_src[...] + rc3_buf[0] + rc3_buf[1] + rc3_buf[2]
    for one in rs:
        one.wait_recv()
    value = own_part[0]
    for d in range(2):
        value += rs_buf[d].astype(F32)
    for i in range(2):
        line = jnp.concatenate([tile[2 * j + i : 2 * j + i + 1, :] for j in range(4)], axis=1)
        here = iota((ROWS, D), 0) + x * ROWS == coarse_ref[0, i]
        value += jnp.where(here, line, 0.0)
    grad_ref[...] += dot_t(value.astype(BF16), weight(1))

    for one in c1 + list(w1.values()) + lat_copies + w2a + w2b + w3a + w3b:
        one.wait_send()
    for one in halo_copies + c3 + c3b + rca + rc1 + hb + rs_far + rs + rc3:
        one.wait_send()
    for d in order:
        c2(d).wait_send()
        rc2(d).wait_send()


def body(node, edge, weights, biases, gains, shifts, halo_send, halo_count, coarse, esend, erecv, cot):
    vmem = pl.BlockSpec(memory_space=pltpu.VMEM)
    smem = pl.BlockSpec(memory_space=pltpu.SMEM)
    return pl.pallas_call(
        kernel,
        name="layer",
        out_shape=(
            jax.ShapeDtypeStruct((ROWS, D), BF16),
            jax.ShapeDtypeStruct((ROWS, D), F32),
        ),
        in_specs=[smem, smem] + [pl.BlockSpec(memory_space=pl.ANY)] * 10,
        out_specs=(vmem, vmem),
        scratch_shapes=[
            pltpu.VMEM((ROWS, D), BF16),
            pltpu.VMEM((EDGES, D), BF16),
            pltpu.VMEM((4, D), F32),
            pltpu.VMEM((2, D), F32),
            pltpu.VMEM((2, D), F32),
            pltpu.VMEM((1, 4, 64), jnp.int32),
            pltpu.VMEM((EDGES,), jnp.int32),
            pltpu.VMEM((EDGES,), jnp.int32),
            pltpu.VMEM((ROWS, D), BF16),
            pltpu.VMEM((TABLE, D), BF16),
            pltpu.VMEM((TABLE, D), BF16),
            pltpu.VMEM((7, NX, 4, 2, 16, D), BF16),
            pltpu.VMEM((EDGES, TABLE), BF16),
            pltpu.VMEM((TABLE, EDGES), BF16),
            pltpu.VMEM((HALO, PART), BF16),
            pltpu.VMEM((NX, ROWS, D), F32),
            pltpu.VMEM((EDGES, BLOCK), BF16),
            pltpu.VMEM((2, BLOCK, SLOTS), BF16),
            pltpu.VMEM((EDGES, D), F32),
            pltpu.VMEM((EDGES, D), F32),
            pltpu.VMEM((EDGES, 1), F32),
            pltpu.VMEM((EDGES, D), BF16),
            pltpu.VMEM((EDGES, D), BF16),
            pltpu.VMEM((8, 128), F32),
            pltpu.VMEM((3, 8, 128), F32),
            pltpu.VMEM((8, 128), F32),
            pltpu.VMEM((NZ, 8, 128), F32),
            pltpu.VMEM((32, D), BF16),
            pltpu.VMEM((HALO, D), BF16),
            pltpu.VMEM((HALO, D), BF16),
            pltpu.VMEM((HALO, D), BF16),
            pltpu.VMEM((3, ROWS, D), BF16),
            pltpu.VMEM((2, ROWS, D), BF16),
            pltpu.VMEM((2, ROWS // 2, D), BF16),
            pltpu.VMEM((4, 2, 32, D), BF16),
            pltpu.VMEM((4, 32, D), BF16),
            pltpu.VMEM((4, 32, D), F32),
            pltpu.VMEM((4, 32, D), BF16),
            pltpu.VMEM((4, 2, 32, D), BF16),
            pltpu.VMEM((3, 32, D), BF16),
            pltpu.VMEM((NZ, 8, 128), F32),
            pltpu.VMEM((NZ, 8, 128), F32),
            pltpu.VMEM((8, 128), F32),
            pltpu.VMEM((3, 8, 128), F32),
            pltpu.SemaphoreType.DMA((N_SEM,)),
            pltpu.SemaphoreType.DMA((N_SEM,)),
            pltpu.SemaphoreType.DMA((11,)),
            pltpu.SemaphoreType.REGULAR((2,)),
        ],
        compiler_params=pltpu.CompilerParams(
            collective_id=0, has_side_effects=True, vmem_limit_bytes=60 * 2**20
        ),
    )(
        coarse, halo_count, node, edge, weights.reshape(7, 4, 2, 16, D), biases, gains, shifts,
        halo_send, esend, erecv, cot,
    )


def solution(mesh):
    rows = P(("dom", "feat"), None)
    flat = P(("dom", "feat"))
    return jax.shard_map(
        body,
        mesh=mesh,
        in_specs=(
            rows, rows, P(None, "feat", None), P(), P(), P(),
            P("dom", None, None), P("dom", None), P("dom", None), flat, flat, rows,
        ),
        out_specs=(rows, rows),
        check_vma=False,
    )
```

```python
import jax
import jax.numpy as jnp
from jax import lax
from jax.experimental import pallas as pl
from jax.experimental.pallas import tpu as pltpu
from jax.sharding import PartitionSpec as P

MESH = pl.DeviceIdType.MESH
F32, BF16 = jnp.float32, jnp.bfloat16
D = 512
ROWS = 256
EDGES = 768
BLOCK = 128
SLOTS = 384
PART = 1024
HALO = 256
COARSE = 256
TABLE = PART + HALO + COARSE
OFFSETS = (1, -1, 2, -2)
NZ, NY, NX = 16, 4, 4
GROUPS = ((0, 3), (3, 4))
EPS = 1e-05

COUNTS = dict(c1=3, w1=12, lat=3, c2=15, w2=12, halo=4, w3=4, c3=3, c3b=1, hb=4, rs=6, rca=1, rc1=3, rc2=15, rc3=3)
BASE = {}
_total = 0
for _name, _n in COUNTS.items():
    BASE[_name] = _total
    _total += _n
N_SEM = _total


def dot(a, b):
    return jnp.dot(a, b, preferred_element_type=F32)


def dot_t(a, b):
    return lax.dot_general(a, b, (((1,), (1,)), ((), ())), preferred_element_type=F32)


def sigmoid(v):
    return 0.5 + 0.5 * jnp.tanh(0.5 * v)


def onehot(mask):
    return jnp.where(mask, 1.0, 0.0).astype(BF16)


def iota(shape, dim):
    return lax.broadcasted_iota(jnp.int32, shape, dim)


def columns(row):
    wide = jnp.broadcast_to(row.astype(F32), (128, row.shape[1]))
    return wide.T.astype(jnp.int32)


def norm(values):
    centred = values - jnp.mean(values, axis=-1, keepdims=True)
    inv = lax.rsqrt(jnp.mean(centred * centred, axis=-1, keepdims=True) + EPS)
    return centred * inv, inv


def norm_back(scaled, normed, inv):
    return inv * (
        scaled
        - jnp.mean(scaled, axis=-1, keepdims=True)
        - normed * jnp.mean(scaled * normed, axis=-1, keepdims=True)
    )


def kernel(
    coarse_ref, count_ref, node_hbm, edge_hbm, wsh_ref, bias_hbm, gain_hbm, shift_hbm,
    halo_hbm, esend_hbm, erecv_hbm, cot_hbm,
    out_ref, grad_ref,
    node_ref, edge_ref, bias_ref, gain_ref, shift_ref, halo_ref, esend_ref, erecv_ref, cot_ref,
    lat, tab, w, sel, sel_t, hsel, own_part, rsel, rsel_t, hid, normed_e, inv_e, msg, hg,
    c1_src, c1_buf, c2_src, c2_buf, c3_src, halo_src, hb_src, hb_buf, part_src, rs_buf, far_buf, ctab, rca_buf, pair_sum, pair_src,
    rc1_src, rc1_buf, rc2_src, rc2_buf, rc3_src, rc3_buf,
    send_sem, recv_sem, local_sem, met_sem,
):
    dom, x = lax.axis_index("dom"), lax.axis_index("feat")
    z, y, c = dom // 8, (dom // 2) % 4, dom % 2
    yc = dom % 8
    zm = z % 4

    def at_x(d):
        return (dom, (x + d) % NX)

    def at_z(d):
        return (((z + d + NZ) % NZ) * 8 + yc, x)

    def at_y(d):
        return (z * 8 + ((y + d) % NY) * 2 + c, x)

    def at_yc(e):
        return (z * 8 + (yc + e) % 8, x)

    def at_dom(o):
        return ((dom + o + 128) % 128, x)

    other_core = (z * 8 + y * 2 + (1 - c), x)

    def copy(name, number, src, dst, device):
        at = BASE[name] + number
        return pltpu.make_async_remote_copy(
            src_ref=src, dst_ref=dst, send_sem=send_sem.at[at], recv_sem=recv_sem.at[at],
            device_id=device, device_id_type=MESH,
        )

    barrier = pltpu.get_barrier_semaphore()
    for d in (1, 2, 3):
        pl.semaphore_signal(barrier, inc=1, device_id=at_x(d), device_id_type=MESH)
    for e in range(1, 8):
        pl.semaphore_signal(barrier, inc=1, device_id=at_yc(e), device_id_type=MESH)
    for o in OFFSETS:
        pl.semaphore_signal(barrier, inc=1, device_id=at_dom(o), device_id_type=MESH)

    for d in (1, -1, 2, -2):
        pl.semaphore_signal(barrier, inc=1, device_id=at_z(d), device_id_type=MESH)

    fetches = {}
    pairs = dict(
        node=(node_hbm, node_ref), halo=(halo_hbm, halo_ref), esend=(esend_hbm, esend_ref),
        erecv=(erecv_hbm, erecv_ref), edge=(edge_hbm, edge_ref), cot=(cot_hbm, cot_ref),
        bias=(bias_hbm, bias_ref), gain=(gain_hbm, gain_ref), shift=(shift_hbm, shift_ref),
    )
    for number, (name, (source, target)) in enumerate(pairs.items()):
        fetches[name] = pltpu.make_async_copy(source, target, local_sem.at[2 + number])
        fetches[name].start()
    fetches["node"].wait()

    row8 = iota((8, ROWS), 0)
    wanted = jnp.where(row8 % 2 == 0, coarse_ref[0, 0], coarse_ref[0, 1]) - x * ROWS
    picked = dot(onehot(wanted == iota((8, ROWS), 1)), node_ref[...])
    quarter = iota((8, 128), 0) // 2
    tile = jnp.zeros((8, 128), F32)
    for j in range(4):
        tile = jnp.where(quarter == j, picked[:, 128 * j : 128 * j + 128], tile)
    c1_src[...] = tile

    own_rows = pl.ds(pl.multiple_of(x * ROWS, ROWS), ROWS)
    lat[own_rows, :] = node_ref[...]
    pl.semaphore_wait(barrier, 3 + 7 + 4 + 4)

    c1 = [copy("c1", d - 1, c1_src, c1_buf.at[d - 1], at_x(d)) for d in (1, 2, 3)]
    for one in c1:
        one.start()
    pieces = ((y, 0), (zm, 1))
    w1 = {}
    for g, (first, count) in enumerate(GROUPS):
        mats = pl.ds(first, count)
        for t, (j, _) in enumerate(pieces):
            cols = pl.ds(256 * t, 256)
            for d in (2, 1, 3):
                w1[g, t, d] = copy(
                    "w1", (g * 2 + t) * 3 + d - 1,
                    wsh_ref.at[mats, j, c, :, cols], w.at[mats, NX - d, j, c, :, cols], at_x(d),
                )
                w1[g, t, d].start()
    lat_copies = [copy("lat", d - 1, node_hbm, lat.at[own_rows, :], at_x(d)) for d in (2, 1, 3)]
    for one in lat_copies:
        one.start()
    for d in (2, -2):
        pl.semaphore_signal(met_sem.at[0], inc=1, device_id=at_z(d), device_id_type=MESH)
    own = pltpu.make_async_copy(wsh_ref, w.at[:, 0], local_sem.at[0])
    own.start()

    fetches["halo"].wait()
    halo_row = jnp.concatenate([halo_ref[0, k : k + 1, :] for k in range(4)], axis=1)
    lane = iota((1, HALO), 1)
    live = count_ref[0, 0]
    for k in (1, 2, 3):
        live = jnp.where(lane // 64 == k, count_ref[0, k], live)
    halo_row = jnp.where(lane % 64 < live, halo_row, -1)
    halo_col = columns(halo_row)

    pl.semaphore_wait(met_sem.at[0], 2)
    for d in (4, -4):
        pl.semaphore_signal(met_sem.at[1], inc=1, device_id=at_z(d), device_id_type=MESH)

    for one in c1:
        one.wait_recv()
    pl.semaphore_wait(met_sem.at[1], 2)
    total = c1_src[...] + c1_buf[0] + c1_buf[1] + c1_buf[2]
    c2_src[...] = total
    c2_buf[z] = total

    def c2(d):
        at = BASE["c2"] + d - 1
        return pltpu.make_async_remote_copy(
            src_ref=c2_src, dst_ref=c2_buf.at[z],
            send_sem=send_sem.at[at], recv_sem=recv_sem.at[at],
            device_id=at_z(d), device_id_type=MESH,
        )

    order = [8]
    for i in range(1, 8):
        order += [8 - i, 8 + i]
    for d in order:
        c2(d).start()

    fetches["esend"].wait()
    index = esend_ref[...].reshape(1, EDGES)
    m = index - (PART + HALO)
    index = jnp.where(
        m >= 0, PART + HALO + ((m >> 1) & 7) * 32 + (m >> 4) * 2 + (m & 1), index
    )

    def w2_start(g):
        first, count = GROUPS[g]
        mats = pl.ds(first, count)
        started = []
        for t, (j, _) in enumerate(pieces):
            cols = pl.ds(256 * t, 256)
            for d in (1, 2, 3):
                w1[g, t, d].wait_recv()
            for d in (2, 1, 3):
                step = d if d < 3 else -1
                target = at_y(d) if t == 0 else at_z(step)
                part = w.at[mats, pl.ds(1, 3), j, c, :, cols]
                one = copy("w2", (g * 2 + t) * 3 + d - 1, part, part, target)
                one.start()
                started.append(one)
        return started

    def w3_start(g, arrived):
        first, count = GROUPS[g]
        mats = pl.ds(first, count)
        started = []
        for t in range(2):
            for one in arrived[3 * t : 3 * t + 3]:
                one.wait_recv()
            part = w.at[mats, pl.ds(1, 3), :, c, :, pl.ds(256 * t, 256)]
            one = copy("w3", g * 2 + t, part, part, other_core)
            one.start()
            started.append(one)
        return started

    w2a = w2_start(0)
    index_col = columns(index)
    for j in range(TABLE // 128):
        sel[:, 128 * j : 128 * j + 128] = onehot(index_col == iota((EDGES, 128), 1) + 128 * j)
    w2b = w2_start(1)
    fetches["erecv"].wait()
    recv_row = erecv_ref[...].reshape(1, EDGES)
    recv_col = columns(recv_row)
    rsel[...] = onehot(recv_col == iota((EDGES, 128), 1))
    for b in range(2):
        rsel_t[b] = onehot(
            iota((BLOCK, SLOTS), 0) == recv_row[:, SLOTS * b : SLOTS * b + SLOTS]
        )

    for j in range(PART // 128):
        hsel[:, 128 * j : 128 * j + 128] = onehot(halo_col == iota((HALO, 128), 1) + 128 * j)
    for j in range(TABLE // 128):
        sel_t[128 * j : 128 * j + 128, :] = onehot(iota((128, EDGES), 0) + 128 * j == index)
    for d in order:
        c2(d).wait_recv()
    flat = c2_buf[...].reshape(NZ * 8, 128).astype(BF16)
    parts = []
    for j in range(4):
        row = iota((32, 128), 0)
        parts.append(dot(onehot((row // 2) * 8 + 2 * j + row % 2 == iota((32, 128), 1)), flat))
    own_coarse = jnp.concatenate(parts, axis=1).astype(BF16)
    c3_src[...] = own_coarse
    ctab[y, c] = own_coarse
    c3 = [copy("c3", d - 1, c3_src, ctab.at[y, c], at_y(d)) for d in (2, 1, 3)]
    for one in c3:
        one.start()
    w3a = w3_start(0, w2a)
    for one in lat_copies:
        one.wait_recv()
    halo_src[...] = dot(hsel[...], lat[:PART, :]).astype(BF16)
    halo_copies = []
    for k in range(4):
        one = copy(
            "halo", k, halo_src.at[pl.ds(64 * k, 64)], lat.at[pl.ds(PART + 64 * k, 64)], at_dom(OFFSETS[k])
        )
        one.start()
        halo_copies.append(one)

    for one in c3:
        one.wait_recv()
    c3b = [copy("c3b", 0, ctab.at[:, c], ctab.at[:, c], other_core)]
    c3b[0].start()
    w3b = w3_start(1, w2b)

    def weight(i):
        return jnp.concatenate(
            [w[i, (k - x + NX) % NX].reshape(D // NX, D) for k in range(NX)], axis=0
        )

    own.wait()

    for name in ("edge", "cot", "bias", "gain", "shift"):
        fetches[name].wait()
    for one in w3a:
        one.wait_recv()
    w_e, w_s, w_r = weight(0), weight(1), weight(2)
    recv_proj = dot(node_ref[...], w_r).astype(BF16)
    for j in range(4):
        rows = slice(256 * j, 256 * j + 256)
        tab[rows, :] = dot(lat[rows, :], w_s).astype(BF16)
    for b in range(2):
        rows = slice(SLOTS * b, SLOTS * b + SLOTS)
        hid[rows, :] = (
            dot(edge_ref[rows, :], w_e)
            + dot(rsel[rows, :], recv_proj[BLOCK * b : BLOCK * b + BLOCK])
            + dot(sel[rows, :PART], tab[:PART, :])
            + bias_ref[0:1, :]
        )
    for one in c3b:
        one.wait_recv()
    rows = slice(PART + HALO, TABLE)
    tab[rows, :] = dot(ctab[...].reshape(COARSE, D), w_s).astype(BF16)
    hid[...] += dot(sel[:, PART + HALO :], tab[rows, :])
    for one in w3b:
        one.wait_recv()
    node = node_ref[...]
    own_part[0] = dot(node, weight(4)) + bias_ref[2:3, :]
    for one in halo_copies:
        one.wait_recv()
    rows = slice(PART, PART + HALO)
    tab[rows, :] = dot(lat[rows, :], w_s).astype(BF16)

    aggregate = []
    for b in range(2):
        rows = slice(SLOTS * b, SLOTS * b + SLOTS)
        h = hid[rows, :] + dot(sel[rows, PART : PART + HALO], tab[PART : PART + HALO, :])
        s = sigmoid(h)
        act = (h * s).astype(BF16)
        hid[rows, :] = s * (1.0 + h * (1.0 - s))
        normed, inv = norm(dot(act, weight(3)) + bias_ref[1:2, :])
        normed_e[rows, :] = normed
        inv_e[rows, :] = inv
        msg[rows, :] = (normed * gain_ref[0:1, :] + shift_ref[0:1, :]).astype(BF16)
        aggregate.append(dot(rsel_t[b], msg[rows, :]).astype(BF16))
    aggregate = jnp.concatenate(aggregate, axis=0)
    node_in = own_part[0] + dot(aggregate, weight(5))
    s = sigmoid(node_in)
    slope = s * (1.0 + node_in * (1.0 - s))
    normed, inv = norm(dot((node_in * s).astype(BF16), weight(6)) + bias_ref[3:4, :])
    out_ref[...] = (
        node.astype(F32) + (normed * gain_ref[1:2, :] + shift_ref[1:2, :])
    ).astype(BF16)
    cot = cot_ref[...].astype(F32)
    node_back = norm_back(cot * gain_ref[1:2, :], normed, inv).astype(BF16)
    node_in_grad = (dot_t(node_back, weight(6)) * slope).astype(BF16)
    agg_grad = dot_t(node_in_grad, weight(5)).astype(BF16)
    for b in range(2):
        rows = slice(SLOTS * b, SLOTS * b + SLOTS)
        back = dot(rsel[rows, :], agg_grad[BLOCK * b : BLOCK * b + BLOCK])
        edge_back = norm_back(back * gain_ref[0:1, :], normed_e[rows, :], inv_e[rows, :]).astype(BF16)
        hg[rows, :] = (dot_t(edge_back, weight(3)) * hid[rows, :]).astype(BF16)

    hb_src[...] = dot(sel_t[PART : PART + HALO, :], hg[...]).astype(BF16)
    hb = []
    for k in range(4):
        part = pl.ds(64 * k, 64)
        hb.append(copy("hb", k, hb_src.at[part], hb_buf.at[part], at_dom(-OFFSETS[k])))
        hb[-1].start()
    rc1_src[...] = dot(sel_t[PART + HALO :, :], hg[...]).astype(BF16).reshape(4, 2, 32, D)
    rca = [copy("rca", 0, rc1_src.at[:, 1 - c], rca_buf, other_core)]
    rca[0].start()

    starts = [pl.multiple_of(((x + d) % NX) * ROWS, ROWS) for d in range(NX)]
    for d in (2, 1, 3, 0):
        own_part[d] = dot(sel_t[pl.ds(starts[d], ROWS), :], hg[...])
    for one in rca:
        one.wait_recv()
    pair_sum[...] = rc1_src[:, c].astype(F32) + rca_buf[...].astype(F32)
    pair_src[...] = pair_sum[...].astype(BF16)
    rc1 = [copy("rc1", d - 1, pair_src.at[(y + d) % NY], rc1_buf.at[d - 1], at_y(d)) for d in (2, 1, 3)]
    for one in rc1:
        one.start()
    recv_grad = [
        dot(rsel_t[b], hg[SLOTS * b : SLOTS * b + SLOTS, :]).astype(BF16) for b in range(2)
    ]
    grad_ref[...] = (
        cot_ref[...].astype(F32)
        + dot_t(node_in_grad, weight(4))
        + dot_t(jnp.concatenate(recv_grad, axis=0), weight(2))
    )

    for one in hb:
        one.wait_recv()
    half = ROWS // 2

    def with_halo(d):
        place = onehot(iota((ROWS, HALO), 0) + starts[d] == halo_row)
        return own_part[d] + dot(place, hb_buf[...])

    low, high = pl.ds(0, half), pl.ds(half, half)

    def rs_send(number, source, target, d):
        one = copy("rs", number, source, target, at_x(d))
        one.start()
        return one

    part_src[2] = with_halo(2).astype(BF16)
    rs_far = [
        rs_send(0, part_src.at[2, low], far_buf.at[0], 1),
        rs_send(1, part_src.at[2, high], far_buf.at[1], 3),
    ]
    next_sum, last_sum = with_halo(1), with_halo(3)
    own_part[1], own_part[3] = next_sum, last_sum
    part_src[0, high] = next_sum[half:].astype(BF16)
    part_src[1, low] = last_sum[:half].astype(BF16)
    rs = [
        rs_send(2, part_src.at[0, high], rs_buf.at[0, high], 1),
        rs_send(3, part_src.at[1, low], rs_buf.at[1, low], 3),
    ]

    for one in rc1:
        one.wait_recv()
    gathered = pair_sum[y]
    for e in range(3):
        gathered += rc1_buf[e].astype(F32)
    gathered = gathered.astype(BF16)
    spread = jnp.zeros((NZ * 8, 128), F32)
    for j in range(4):
        row, col = iota((NZ * 8, 32), 0), iota((NZ * 8, 32), 1)
        place = (row // 8 == col // 2) & (row % 8 == 2 * j + col % 2)
        spread += dot(onehot(place), gathered[:, 128 * j : 128 * j + 128])
    rc2_src[...] = spread.reshape(NZ, 8, 128)
    rc2_buf[z] = rc2_src[z]

    def rc2(d):
        at = BASE["rc2"] + d - 1
        return pltpu.make_async_remote_copy(
            src_ref=rc2_src.at[(z + d) % NZ], dst_ref=rc2_buf.at[z],
            send_sem=send_sem.at[at], recv_sem=recv_sem.at[at],
            device_id=at_z(d), device_id_type=MESH,
        )

    for d in order:
        rc2(d).start()

    own_part[0] = with_halo(0)
    for one in rs_far:
        one.wait_recv()
    part_src[0, low] = (own_part[1, low] + far_buf[0].astype(F32)).astype(BF16)
    rs.append(rs_send(4, part_src.at[0, low], rs_buf.at[0, low], 1))
    part_src[1, high] = (own_part[3, high] + far_buf[1].astype(F32)).astype(BF16)
    rs.append(rs_send(5, part_src.at[1, high], rs_buf.at[1, high], 3))

    for d in order:
        rc2(d).wait_recv()
    tile = jnp.sum(rc2_buf[...], axis=0)
    rc3_src[...] = tile
    rc3 = [copy("rc3", d - 1, rc3_src, rc3_buf.at[d - 1], at_x(d)) for d in (1, 2, 3)]
    for one in rc3:
        one.start()
    for one in rc3:
        one.wait_recv()
    tile = rc3_src[...] + rc3_buf[0] + rc3_buf[1] + rc3_buf[2]
    for one in rs:
        one.wait_recv()
    value = own_part[0]
    for d in range(2):
        value += rs_buf[d].astype(F32)
    for i in range(2):
        line = jnp.concatenate([tile[2 * j + i : 2 * j + i + 1, :] for j in range(4)], axis=1)
        here = iota((ROWS, D), 0) + x * ROWS == coarse_ref[0, i]
        value += jnp.where(here, line, 0.0)
    grad_ref[...] += dot_t(value.astype(BF16), weight(1))

    for one in c1 + list(w1.values()) + lat_copies + w2a + w2b + w3a + w3b:
        one.wait_send()
    for one in halo_copies + c3 + c3b + rca + rc1 + hb + rs_far + rs + rc3:
        one.wait_send()
    for d in order:
        c2(d).wait_send()
        rc2(d).wait_send()


def body(node, edge, weights, biases, gains, shifts, halo_send, halo_count, coarse, esend, erecv, cot):
    vmem = pl.BlockSpec(memory_space=pltpu.VMEM)
    smem = pl.BlockSpec(memory_space=pltpu.SMEM)
    return pl.pallas_call(
        kernel,
        name="layer",
        out_shape=(
            jax.ShapeDtypeStruct((ROWS, D), BF16),
            jax.ShapeDtypeStruct((ROWS, D), F32),
        ),
        in_specs=[smem, smem] + [pl.BlockSpec(memory_space=pl.ANY)] * 10,
        out_specs=(vmem, vmem),
        scratch_shapes=[
            pltpu.VMEM((ROWS, D), BF16),
            pltpu.VMEM((EDGES, D), BF16),
            pltpu.VMEM((4, D), F32),
            pltpu.VMEM((2, D), F32),
            pltpu.VMEM((2, D), F32),
            pltpu.VMEM((1, 4, 64), jnp.int32),
            pltpu.VMEM((EDGES,), jnp.int32),
            pltpu.VMEM((EDGES,), jnp.int32),
            pltpu.VMEM((ROWS, D), BF16),
            pltpu.VMEM((TABLE, D), BF16),
            pltpu.VMEM((TABLE, D), BF16),
            pltpu.VMEM((7, NX, 4, 2, 16, D), BF16),
            pltpu.VMEM((EDGES, TABLE), BF16),
            pltpu.VMEM((TABLE, EDGES), BF16),
            pltpu.VMEM((HALO, PART), BF16),
            pltpu.VMEM((NX, ROWS, D), F32),
            pltpu.VMEM((EDGES, BLOCK), BF16),
            pltpu.VMEM((2, BLOCK, SLOTS), BF16),
            pltpu.VMEM((EDGES, D), F32),
            pltpu.VMEM((EDGES, D), F32),
            pltpu.VMEM((EDGES, 1), F32),
            pltpu.VMEM((EDGES, D), BF16),
            pltpu.VMEM((EDGES, D), BF16),
            pltpu.VMEM((8, 128), F32),
            pltpu.VMEM((3, 8, 128), F32),
            pltpu.VMEM((8, 128), F32),
            pltpu.VMEM((NZ, 8, 128), F32),
            pltpu.VMEM((32, D), BF16),
            pltpu.VMEM((HALO, D), BF16),
            pltpu.VMEM((HALO, D), BF16),
            pltpu.VMEM((HALO, D), BF16),
            pltpu.VMEM((3, ROWS, D), BF16),
            pltpu.VMEM((2, ROWS, D), BF16),
            pltpu.VMEM((2, ROWS // 2, D), BF16),
            pltpu.VMEM((4, 2, 32, D), BF16),
            pltpu.VMEM((4, 32, D), BF16),
            pltpu.VMEM((4, 32, D), F32),
            pltpu.VMEM((4, 32, D), BF16),
            pltpu.VMEM((4, 2, 32, D), BF16),
            pltpu.VMEM((3, 32, D), BF16),
            pltpu.VMEM((NZ, 8, 128), F32),
            pltpu.VMEM((NZ, 8, 128), F32),
            pltpu.VMEM((8, 128), F32),
            pltpu.VMEM((3, 8, 128), F32),
            pltpu.SemaphoreType.DMA((N_SEM,)),
            pltpu.SemaphoreType.DMA((N_SEM,)),
            pltpu.SemaphoreType.DMA((11,)),
            pltpu.SemaphoreType.REGULAR((2,)),
        ],
        compiler_params=pltpu.CompilerParams(
            collective_id=0, has_side_effects=True, vmem_limit_bytes=60 * 2**20
        ),
    )(
        coarse, halo_count, node, edge, weights.reshape(7, 4, 2, 16, D), biases, gains, shifts,
        halo_send, esend, erecv, cot,
    )


def solution(mesh):
    rows = P(("dom", "feat"), None)
    flat = P(("dom", "feat"))
    return jax.shard_map(
        body,
        mesh=mesh,
        in_specs=(
            rows, rows, P(None, "feat", None), P(), P(), P(),
            P("dom", None, None), P("dom", None), P("dom", None), flat, flat, rows,
        ),
        out_specs=(rows, rows),
        check_vma=False,
    )
```

```python
import jax
import jax.numpy as jnp
from jax import lax
from jax.experimental import pallas as pl
from jax.experimental.pallas import tpu as pltpu
from jax.sharding import PartitionSpec as P

MESH = pl.DeviceIdType.MESH
F32, BF16 = jnp.float32, jnp.bfloat16
D = 512
ROWS = 256
EDGES = 768
BLOCK = 128
SLOTS = 384
PART = 1024
HALO = 256
COARSE = 256
TABLE = PART + HALO + COARSE
OFFSETS = (1, -1, 2, -2)
NZ, NY, NX = 16, 4, 4
GROUPS = ((0, 3), (3, 4))
EPS = 1e-05

COUNTS = dict(c1=3, w1=12, lat=3, c2=15, w2=12, halo=4, w3=4, c3=3, c3b=1, hb=4, rs=6, rca=1, rc1=3, rc2=15, rc3=3)
BASE = {}
_total = 0
for _name, _n in COUNTS.items():
    BASE[_name] = _total
    _total += _n
N_SEM = _total


def dot(a, b):
    return jnp.dot(a, b, preferred_element_type=F32)


def dot_t(a, b):
    return lax.dot_general(a, b, (((1,), (1,)), ((), ())), preferred_element_type=F32)


def sigmoid(v):
    return 0.5 + 0.5 * jnp.tanh(0.5 * v)


def onehot(mask):
    return jnp.where(mask, 1.0, 0.0).astype(BF16)


def iota(shape, dim):
    return lax.broadcasted_iota(jnp.int32, shape, dim)


def columns(row):
    wide = jnp.broadcast_to(row.astype(F32), (128, row.shape[1]))
    return wide.T.astype(jnp.int32)


def norm(values):
    centred = values - jnp.mean(values, axis=-1, keepdims=True)
    inv = lax.rsqrt(jnp.mean(centred * centred, axis=-1, keepdims=True) + EPS)
    return centred * inv, inv


def norm_back(scaled, normed, inv):
    return inv * (
        scaled
        - jnp.mean(scaled, axis=-1, keepdims=True)
        - normed * jnp.mean(scaled * normed, axis=-1, keepdims=True)
    )


def kernel(
    coarse_ref, count_ref, node_hbm, edge_hbm, wsh_ref, bias_hbm, gain_hbm, shift_hbm,
    halo_hbm, esend_hbm, erecv_hbm, cot_hbm,
    out_ref, grad_ref,
    node_ref, edge_ref, bias_ref, gain_ref, shift_ref, halo_ref, esend_ref, erecv_ref, cot_ref,
    lat, tab, w, sel, sel_t, hsel, own_part, rsel, rsel_t, hid, normed_e, inv_e, msg, hg,
    c1_src, c1_buf, c2_src, c2_buf, c3_src, halo_src, hb_src, hb_buf, part_src, rs_buf, far_buf, ctab, rca_buf, pair_sum, pair_src,
    rc1_src, rc1_buf, rc2_src, rc2_buf, rc3_src, rc3_buf,
    send_sem, recv_sem, local_sem, met_sem,
):
    dom, x = lax.axis_index("dom"), lax.axis_index("feat")
    z, y, c = dom // 8, (dom // 2) % 4, dom % 2
    yc = dom % 8
    zm = z % 4

    def at_x(d):
        return (dom, (x + d) % NX)

    def at_z(d):
        return (((z + d + NZ) % NZ) * 8 + yc, x)

    def at_y(d):
        return (z * 8 + ((y + d) % NY) * 2 + c, x)

    def at_yc(e):
        return (z * 8 + (yc + e) % 8, x)

    def at_dom(o):
        return ((dom + o + 128) % 128, x)

    other_core = (z * 8 + y * 2 + (1 - c), x)

    def copy(name, number, src, dst, device):
        at = BASE[name] + number
        return pltpu.make_async_remote_copy(
            src_ref=src, dst_ref=dst, send_sem=send_sem.at[at], recv_sem=recv_sem.at[at],
            device_id=device, device_id_type=MESH,
        )

    barrier = pltpu.get_barrier_semaphore()
    for d in (1, 2, 3):
        pl.semaphore_signal(barrier, inc=1, device_id=at_x(d), device_id_type=MESH)
    for e in range(1, 8):
        pl.semaphore_signal(barrier, inc=1, device_id=at_yc(e), device_id_type=MESH)
    for o in OFFSETS:
        pl.semaphore_signal(barrier, inc=1, device_id=at_dom(o), device_id_type=MESH)

    for d in (1, -1, 2, -2):
        pl.semaphore_signal(barrier, inc=1, device_id=at_z(d), device_id_type=MESH)

    fetches = {}
    pairs = dict(
        node=(node_hbm, node_ref), halo=(halo_hbm, halo_ref), esend=(esend_hbm, esend_ref),
        erecv=(erecv_hbm, erecv_ref), edge=(edge_hbm, edge_ref), cot=(cot_hbm, cot_ref),
        bias=(bias_hbm, bias_ref), gain=(gain_hbm, gain_ref), shift=(shift_hbm, shift_ref),
    )
    for number, (name, (source, target)) in enumerate(pairs.items()):
        fetches[name] = pltpu.make_async_copy(source, target, local_sem.at[2 + number])
        fetches[name].start()
    fetches["node"].wait()

    row8 = iota((8, ROWS), 0)
    wanted = jnp.where(row8 % 2 == 0, coarse_ref[0, 0], coarse_ref[0, 1]) - x * ROWS
    picked = dot(onehot(wanted == iota((8, ROWS), 1)), node_ref[...])
    quarter = iota((8, 128), 0) // 2
    tile = jnp.zeros((8, 128), F32)
    for j in range(4):
        tile = jnp.where(quarter == j, picked[:, 128 * j : 128 * j + 128], tile)
    c1_src[...] = tile

    own_rows = pl.ds(pl.multiple_of(x * ROWS, ROWS), ROWS)
    lat[own_rows, :] = node_ref[...]
    pl.semaphore_wait(barrier, 3 + 7 + 4 + 4)

    c1 = [copy("c1", d - 1, c1_src, c1_buf.at[d - 1], at_x(d)) for d in (1, 2, 3)]
    for one in c1:
        one.start()
    pieces = ((y, 0), (zm, 1))
    w1 = {}
    for g, (first, count) in enumerate(GROUPS):
        mats = pl.ds(first, count)
        for t, (j, _) in enumerate(pieces):
            cols = pl.ds(256 * t, 256)
            for d in (2, 1, 3):
                w1[g, t, d] = copy(
                    "w1", (g * 2 + t) * 3 + d - 1,
                    wsh_ref.at[mats, j, c, :, cols], w.at[mats, NX - d, j, c, :, cols], at_x(d),
                )
                w1[g, t, d].start()
    lat_copies = [copy("lat", d - 1, node_hbm, lat.at[own_rows, :], at_x(d)) for d in (2, 1, 3)]
    for one in lat_copies:
        one.start()
    for d in (2, -2):
        pl.semaphore_signal(met_sem.at[0], inc=1, device_id=at_z(d), device_id_type=MESH)
    own = pltpu.make_async_copy(wsh_ref, w.at[:, 0], local_sem.at[0])
    own.start()

    fetches["halo"].wait()
    halo_row = jnp.concatenate([halo_ref[0, k : k + 1, :] for k in range(4)], axis=1)
    lane = iota((1, HALO), 1)
    live = count_ref[0, 0]
    for k in (1, 2, 3):
        live = jnp.where(lane // 64 == k, count_ref[0, k], live)
    halo_row = jnp.where(lane % 64 < live, halo_row, -1)
    halo_col = columns(halo_row)

    pl.semaphore_wait(met_sem.at[0], 2)
    for d in (4, -4):
        pl.semaphore_signal(met_sem.at[1], inc=1, device_id=at_z(d), device_id_type=MESH)

    for one in c1:
        one.wait_recv()
    pl.semaphore_wait(met_sem.at[1], 2)
    total = c1_src[...] + c1_buf[0] + c1_buf[1] + c1_buf[2]
    c2_src[...] = total
    c2_buf[z] = total

    def c2(d):
        at = BASE["c2"] + d - 1
        return pltpu.make_async_remote_copy(
            src_ref=c2_src, dst_ref=c2_buf.at[z],
            send_sem=send_sem.at[at], recv_sem=recv_sem.at[at],
            device_id=at_z(d), device_id_type=MESH,
        )

    order = [8]
    for i in range(1, 8):
        order += [8 - i, 8 + i]
    for d in order:
        c2(d).start()

    fetches["esend"].wait()
    index = esend_ref[...].reshape(1, EDGES)
    m = index - (PART + HALO)
    index = jnp.where(
        m >= 0, PART + HALO + ((m >> 1) & 7) * 32 + (m >> 4) * 2 + (m & 1), index
    )

    def w2_start(g):
        first, count = GROUPS[g]
        mats = pl.ds(first, count)
        started = []
        for t, (j, _) in enumerate(pieces):
            cols = pl.ds(256 * t, 256)
            for d in (1, 2, 3):
                w1[g, t, d].wait_recv()
            for d in (2, 1, 3):
                step = d if d < 3 else -1
                target = at_y(d) if t == 0 else at_z(step)
                part = w.at[mats, pl.ds(1, 3), j, c, :, cols]
                one = copy("w2", (g * 2 + t) * 3 + d - 1, part, part, target)
                one.start()
                started.append(one)
        return started

    def w3_start(g, arrived):
        first, count = GROUPS[g]
        mats = pl.ds(first, count)
        started = []
        for t in range(2):
            for one in arrived[3 * t : 3 * t + 3]:
                one.wait_recv()
            part = w.at[mats, pl.ds(1, 3), :, c, :, pl.ds(256 * t, 256)]
            one = copy("w3", g * 2 + t, part, part, other_core)
            one.start()
            started.append(one)
        return started

    w2a = w2_start(0)
    w2b = w2_start(1)
    index_col = columns(index)
    for j in range(TABLE // 128):
        sel[:, 128 * j : 128 * j + 128] = onehot(index_col == iota((EDGES, 128), 1) + 128 * j)
    fetches["erecv"].wait()
    recv_row = erecv_ref[...].reshape(1, EDGES)
    recv_col = columns(recv_row)
    rsel[...] = onehot(recv_col == iota((EDGES, 128), 1))
    for b in range(2):
        rsel_t[b] = onehot(
            iota((BLOCK, SLOTS), 0) == recv_row[:, SLOTS * b : SLOTS * b + SLOTS]
        )

    for j in range(PART // 128):
        hsel[:, 128 * j : 128 * j + 128] = onehot(halo_col == iota((HALO, 128), 1) + 128 * j)
    for j in range(TABLE // 128):
        sel_t[128 * j : 128 * j + 128, :] = onehot(iota((128, EDGES), 0) + 128 * j == index)
    for d in order:
        c2(d).wait_recv()
    flat = c2_buf[...].reshape(NZ * 8, 128).astype(BF16)
    parts = []
    for j in range(4):
        row = iota((32, 128), 0)
        parts.append(dot(onehot((row // 2) * 8 + 2 * j + row % 2 == iota((32, 128), 1)), flat))
    own_coarse = jnp.concatenate(parts, axis=1).astype(BF16)
    c3_src[...] = own_coarse
    ctab[y, c] = own_coarse
    c3 = [copy("c3", d - 1, c3_src, ctab.at[y, c], at_y(d)) for d in (2, 1, 3)]
    for one in c3:
        one.start()
    w3a = w3_start(0, w2a)
    for one in lat_copies:
        one.wait_recv()
    halo_src[...] = dot(hsel[...], lat[:PART, :]).astype(BF16)
    halo_copies = []
    for k in range(4):
        one = copy(
            "halo", k, halo_src.at[pl.ds(64 * k, 64)], lat.at[pl.ds(PART + 64 * k, 64)], at_dom(OFFSETS[k])
        )
        one.start()
        halo_copies.append(one)

    for one in c3:
        one.wait_recv()
    c3b = [copy("c3b", 0, ctab.at[:, c], ctab.at[:, c], other_core)]
    c3b[0].start()
    w3b = w3_start(1, w2b)

    def weight(i):
        return jnp.concatenate(
            [w[i, (k - x + NX) % NX].reshape(D // NX, D) for k in range(NX)], axis=0
        )

    own.wait()

    for name in ("edge", "cot", "bias", "gain", "shift"):
        fetches[name].wait()
    for one in w3a:
        one.wait_recv()
    w_e, w_s, w_r = weight(0), weight(1), weight(2)
    recv_proj = dot(node_ref[...], w_r).astype(BF16)
    for j in range(4):
        rows = slice(256 * j, 256 * j + 256)
        tab[rows, :] = dot(lat[rows, :], w_s).astype(BF16)
    for b in range(2):
        rows = slice(SLOTS * b, SLOTS * b + SLOTS)
        hid[rows, :] = (
            dot(edge_ref[rows, :], w_e)
            + dot(rsel[rows, :], recv_proj[BLOCK * b : BLOCK * b + BLOCK])
            + dot(sel[rows, :PART], tab[:PART, :])
            + bias_ref[0:1, :]
        )
    for one in c3b:
        one.wait_recv()
    rows = slice(PART + HALO, TABLE)
    tab[rows, :] = dot(ctab[...].reshape(COARSE, D), w_s).astype(BF16)
    hid[...] += dot(sel[:, PART + HALO :], tab[rows, :])
    for one in w3b:
        one.wait_recv()
    node = node_ref[...]
    own_part[0] = dot(node, weight(4)) + bias_ref[2:3, :]
    for one in halo_copies:
        one.wait_recv()
    rows = slice(PART, PART + HALO)
    tab[rows, :] = dot(lat[rows, :], w_s).astype(BF16)

    aggregate = []
    for b in range(2):
        rows = slice(SLOTS * b, SLOTS * b + SLOTS)
        h = hid[rows, :] + dot(sel[rows, PART : PART + HALO], tab[PART : PART + HALO, :])
        s = sigmoid(h)
        act = (h * s).astype(BF16)
        hid[rows, :] = s * (1.0 + h * (1.0 - s))
        normed, inv = norm(dot(act, weight(3)) + bias_ref[1:2, :])
        normed_e[rows, :] = normed
        inv_e[rows, :] = inv
        msg[rows, :] = (normed * gain_ref[0:1, :] + shift_ref[0:1, :]).astype(BF16)
        aggregate.append(dot(rsel_t[b], msg[rows, :]).astype(BF16))
    aggregate = jnp.concatenate(aggregate, axis=0)
    node_in = own_part[0] + dot(aggregate, weight(5))
    s = sigmoid(node_in)
    slope = s * (1.0 + node_in * (1.0 - s))
    normed, inv = norm(dot((node_in * s).astype(BF16), weight(6)) + bias_ref[3:4, :])
    out_ref[...] = (
        node.astype(F32) + (normed * gain_ref[1:2, :] + shift_ref[1:2, :])
    ).astype(BF16)
    cot = cot_ref[...].astype(F32)
    node_back = norm_back(cot * gain_ref[1:2, :], normed, inv).astype(BF16)
    node_in_grad = (dot_t(node_back, weight(6)) * slope).astype(BF16)
    agg_grad = dot_t(node_in_grad, weight(5)).astype(BF16)
    for b in range(2):
        rows = slice(SLOTS * b, SLOTS * b + SLOTS)
        back = dot(rsel[rows, :], agg_grad[BLOCK * b : BLOCK * b + BLOCK])
        edge_back = norm_back(back * gain_ref[0:1, :], normed_e[rows, :], inv_e[rows, :]).astype(BF16)
        hg[rows, :] = (dot_t(edge_back, weight(3)) * hid[rows, :]).astype(BF16)

    hb_src[...] = dot(sel_t[PART : PART + HALO, :], hg[...]).astype(BF16)
    hb = []
    for k in range(4):
        part = pl.ds(64 * k, 64)
        hb.append(copy("hb", k, hb_src.at[part], hb_buf.at[part], at_dom(-OFFSETS[k])))
        hb[-1].start()
    rc1_src[...] = dot(sel_t[PART + HALO :, :], hg[...]).astype(BF16).reshape(4, 2, 32, D)
    rca = [copy("rca", 0, rc1_src.at[:, 1 - c], rca_buf, other_core)]
    rca[0].start()

    starts = [pl.multiple_of(((x + d) % NX) * ROWS, ROWS) for d in range(NX)]
    for d in (2, 1, 3, 0):
        own_part[d] = dot(sel_t[pl.ds(starts[d], ROWS), :], hg[...])
    for one in rca:
        one.wait_recv()
    pair_sum[...] = rc1_src[:, c].astype(F32) + rca_buf[...].astype(F32)
    pair_src[...] = pair_sum[...].astype(BF16)
    rc1 = [copy("rc1", d - 1, pair_src.at[(y + d) % NY], rc1_buf.at[d - 1], at_y(d)) for d in (2, 1, 3)]
    for one in rc1:
        one.start()
    recv_grad = [
        dot(rsel_t[b], hg[SLOTS * b : SLOTS * b + SLOTS, :]).astype(BF16) for b in range(2)
    ]
    grad_ref[...] = (
        cot_ref[...].astype(F32)
        + dot_t(node_in_grad, weight(4))
        + dot_t(jnp.concatenate(recv_grad, axis=0), weight(2))
    )

    for one in hb:
        one.wait_recv()
    half = ROWS // 2

    def with_halo(d):
        place = onehot(iota((ROWS, HALO), 0) + starts[d] == halo_row)
        return own_part[d] + dot(place, hb_buf[...])

    low, high = pl.ds(0, half), pl.ds(half, half)

    def rs_send(number, source, target, d):
        one = copy("rs", number, source, target, at_x(d))
        one.start()
        return one

    part_src[2] = with_halo(2).astype(BF16)
    rs_far = [
        rs_send(0, part_src.at[2, low], far_buf.at[0], 1),
        rs_send(1, part_src.at[2, high], far_buf.at[1], 3),
    ]
    next_sum, last_sum = with_halo(1), with_halo(3)
    own_part[1], own_part[3] = next_sum, last_sum
    part_src[0, high] = next_sum[half:].astype(BF16)
    part_src[1, low] = last_sum[:half].astype(BF16)
    rs = [
        rs_send(2, part_src.at[0, high], rs_buf.at[0, high], 1),
        rs_send(3, part_src.at[1, low], rs_buf.at[1, low], 3),
    ]

    for one in rc1:
        one.wait_recv()
    gathered = pair_sum[y]
    for e in range(3):
        gathered += rc1_buf[e].astype(F32)
    gathered = gathered.astype(BF16)
    spread = jnp.zeros((NZ * 8, 128), F32)
    for j in range(4):
        row, col = iota((NZ * 8, 32), 0), iota((NZ * 8, 32), 1)
        place = (row // 8 == col // 2) & (row % 8 == 2 * j + col % 2)
        spread += dot(onehot(place), gathered[:, 128 * j : 128 * j + 128])
    rc2_src[...] = spread.reshape(NZ, 8, 128)
    rc2_buf[z] = rc2_src[z]

    def rc2(d):
        at = BASE["rc2"] + d - 1
        return pltpu.make_async_remote_copy(
            src_ref=rc2_src.at[(z + d) % NZ], dst_ref=rc2_buf.at[z],
            send_sem=send_sem.at[at], recv_sem=recv_sem.at[at],
            device_id=at_z(d), device_id_type=MESH,
        )

    for d in order:
        rc2(d).start()

    own_part[0] = with_halo(0)
    for one in rs_far:
        one.wait_recv()
    part_src[0, low] = (own_part[1, low] + far_buf[0].astype(F32)).astype(BF16)
    rs.append(rs_send(4, part_src.at[0, low], rs_buf.at[0, low], 1))
    part_src[1, high] = (own_part[3, high] + far_buf[1].astype(F32)).astype(BF16)
    rs.append(rs_send(5, part_src.at[1, high], rs_buf.at[1, high], 3))

    for d in order:
        rc2(d).wait_recv()
    tile = jnp.sum(rc2_buf[...], axis=0)
    rc3_src[...] = tile
    rc3 = [copy("rc3", d - 1, rc3_src, rc3_buf.at[d - 1], at_x(d)) for d in (1, 2, 3)]
    for one in rc3:
        one.start()
    for one in rc3:
        one.wait_recv()
    tile = rc3_src[...] + rc3_buf[0] + rc3_buf[1] + rc3_buf[2]
    for one in rs:
        one.wait_recv()
    value = own_part[0]
    for d in range(2):
        value += rs_buf[d].astype(F32)
    for i in range(2):
        line = jnp.concatenate([tile[2 * j + i : 2 * j + i + 1, :] for j in range(4)], axis=1)
        here = iota((ROWS, D), 0) + x * ROWS == coarse_ref[0, i]
        value += jnp.where(here, line, 0.0)
    grad_ref[...] += dot_t(value.astype(BF16), weight(1))

    for one in c1 + list(w1.values()) + lat_copies + w2a + w2b + w3a + w3b:
        one.wait_send()
    for one in halo_copies + c3 + c3b + rca + rc1 + hb + rs_far + rs + rc3:
        one.wait_send()
    for d in order:
        c2(d).wait_send()
        rc2(d).wait_send()


def body(node, edge, weights, biases, gains, shifts, halo_send, halo_count, coarse, esend, erecv, cot):
    vmem = pl.BlockSpec(memory_space=pltpu.VMEM)
    smem = pl.BlockSpec(memory_space=pltpu.SMEM)
    return pl.pallas_call(
        kernel,
        name="layer",
        out_shape=(
            jax.ShapeDtypeStruct((ROWS, D), BF16),
            jax.ShapeDtypeStruct((ROWS, D), F32),
        ),
        in_specs=[smem, smem] + [pl.BlockSpec(memory_space=pl.ANY)] * 10,
        out_specs=(vmem, vmem),
        scratch_shapes=[
            pltpu.VMEM((ROWS, D), BF16),
            pltpu.VMEM((EDGES, D), BF16),
            pltpu.VMEM((4, D), F32),
            pltpu.VMEM((2, D), F32),
            pltpu.VMEM((2, D), F32),
            pltpu.VMEM((1, 4, 64), jnp.int32),
            pltpu.VMEM((EDGES,), jnp.int32),
            pltpu.VMEM((EDGES,), jnp.int32),
            pltpu.VMEM((ROWS, D), BF16),
            pltpu.VMEM((TABLE, D), BF16),
            pltpu.VMEM((TABLE, D), BF16),
            pltpu.VMEM((7, NX, 4, 2, 16, D), BF16),
            pltpu.VMEM((EDGES, TABLE), BF16),
            pltpu.VMEM((TABLE, EDGES), BF16),
            pltpu.VMEM((HALO, PART), BF16),
            pltpu.VMEM((NX, ROWS, D), F32),
            pltpu.VMEM((EDGES, BLOCK), BF16),
            pltpu.VMEM((2, BLOCK, SLOTS), BF16),
            pltpu.VMEM((EDGES, D), F32),
            pltpu.VMEM((EDGES, D), F32),
            pltpu.VMEM((EDGES, 1), F32),
            pltpu.VMEM((EDGES, D), BF16),
            pltpu.VMEM((EDGES, D), BF16),
            pltpu.VMEM((8, 128), F32),
            pltpu.VMEM((3, 8, 128), F32),
            pltpu.VMEM((8, 128), F32),
            pltpu.VMEM((NZ, 8, 128), F32),
            pltpu.VMEM((32, D), BF16),
            pltpu.VMEM((HALO, D), BF16),
            pltpu.VMEM((HALO, D), BF16),
            pltpu.VMEM((HALO, D), BF16),
            pltpu.VMEM((3, ROWS, D), BF16),
            pltpu.VMEM((2, ROWS, D), BF16),
            pltpu.VMEM((2, ROWS // 2, D), BF16),
            pltpu.VMEM((4, 2, 32, D), BF16),
            pltpu.VMEM((4, 32, D), BF16),
            pltpu.VMEM((4, 32, D), F32),
            pltpu.VMEM((4, 32, D), BF16),
            pltpu.VMEM((4, 2, 32, D), BF16),
            pltpu.VMEM((3, 32, D), BF16),
            pltpu.VMEM((NZ, 8, 128), F32),
            pltpu.VMEM((NZ, 8, 128), F32),
            pltpu.VMEM((8, 128), F32),
            pltpu.VMEM((3, 8, 128), F32),
            pltpu.SemaphoreType.DMA((N_SEM,)),
            pltpu.SemaphoreType.DMA((N_SEM,)),
            pltpu.SemaphoreType.DMA((11,)),
            pltpu.SemaphoreType.REGULAR((2,)),
        ],
        compiler_params=pltpu.CompilerParams(
            collective_id=0, has_side_effects=True, vmem_limit_bytes=60 * 2**20
        ),
    )(
        coarse, halo_count, node, edge, weights.reshape(7, 4, 2, 16, D), biases, gains, shifts,
        halo_send, esend, erecv, cot,
    )


def solution(mesh):
    rows = P(("dom", "feat"), None)
    flat = P(("dom", "feat"))
    return jax.shard_map(
        body,
        mesh=mesh,
        in_specs=(
            rows, rows, P(None, "feat", None), P(), P(), P(),
            P("dom", None, None), P("dom", None), P("dom", None), flat, flat, rows,
        ),
        out_specs=(rows, rows),
        check_vma=False,
    )
```
